256 devices in a mesh: row: 16 (over y, x_lo, core), col: 16 (over x_hi, z).
Axes of the slice: x: 4 (x_hi: 2, x_lo: 2; x = x_hi * 2 + x_lo), y: 4, z: 8, core: 2. Of those that a mesh axis runs over, the one named last changes fastest.
Arguments:
- features: bfloat16 [131072, 128], P(('row', 'col')), may hold values from -6 to 6
- weight: bfloat16 [128, 256], replicated, may hold values from -0.5 to 0.5
- grad_out: bfloat16 [131072, 256], P(('row', 'col')), may hold values from -6 to 6
- tile_rows: int32 [16, 16, 48], P('row', 'col'), may hold values from 0 to 63
- tile_cols: int32 [16, 16, 48], P('row', 'col'), may hold values from 0 to 63
- tile_vals: bfloat16 [16, 16, 48, 128, 128], P('row', 'col'), as said below
- tile_count: int32 [16, 16], P('row', 'col'), may hold values from 12 to 48, as said below
Outputs:
- activation: bfloat16 [131072, 256], P(('row', 'col'))
- grad_features: bfloat16 [131072, 128], P(('row', 'col'))
- grad_weight: float32 [128, 256], replicated
The draws below stay inside these ranges and needn't reach their ends.
Inputs may be any that keep to these rules, and one draw needn't show every extreme that they name: `tile_count`: one device holds exactly 48 live slots. `tile_vals`: each entry of a tile is nonzero with probability 2 / 128.
All inputs are finite; a program needn't handle non-finite values.
Results may differ from the reference program's by a relative error of at most 0.006.
Values may be sent and summed in bfloat16 or wider, within the bound.
No kernel may reach another device: no remote copies, remote signals or barrier semaphores. Data moves between devices by JAX's collectives and lax.ppermute only.
A program may use at most 64 MiB of HBM per device.

```python
import jax
import jax.numpy as jnp
from jax import lax

FEAT = 128
HIDDEN_SIZE = 256
BLOCK = 128
NODE_DEV = 512
NT = 48
PROWS = 16
PCOLS = 16
NODES = 131072
ROW_BLOCKS = 64
COL_BLOCKS = 64


def draw_tile_count(key, part):
    key = jax.random.fold_in(key, 5)
    first, second = jax.random.split(key)
    counts = jax.random.randint(first, (PROWS * PCOLS,), NT // 4, NT + 1)
    chosen = jax.random.randint(second, (), 0, PROWS * PCOLS)
    counts = jnp.where(jnp.arange(PROWS * PCOLS) == chosen, NT, counts)
    return counts.reshape(PROWS, PCOLS).astype(jnp.int32)


def draw_tile_vals(key, part):
    key = jax.random.fold_in(key, 9)
    first, second = jax.random.split(key)
    shape = (PROWS, PCOLS, NT, BLOCK, BLOCK)
    present = (jax.random.uniform(first, shape, jnp.float32) < 2.0 / BLOCK).astype(jnp.float32)
    values = jax.random.normal(second, shape, jnp.float32)
    degree = max(1.0, 2.0 * NT * BLOCK / NODE_DEV)
    return (values * present / degree ** 0.5).astype(jnp.bfloat16)


def set_ends(result, stream_key, smallest, largest):
    shape = result.shape
    place = [jax.random.randint(jax.random.fold_in(stream_key, axis), (), 0, shape[axis]) for axis in range(len(shape))]
    result = result.at[tuple(place)].set(smallest)
    longest = shape.index(max(shape))
    place[longest] = (place[longest] + 1) % shape[longest]
    return result.at[tuple(place)].set(largest)


def shard_levels(rng, dims, cuts, low, largest):
    factor_of, own = 1.0, jax.random.fold_in(rng, 6)
    for position, parts in cuts:
        draws = jnp.exp(jax.random.uniform(jax.random.fold_in(own, position), (parts,), jnp.float32, low / len(cuts), largest / len(cuts)))
        factor_of = factor_of * jnp.repeat(draws, dims[position] // parts).reshape([-1 if axis == position else 1 for axis in range(len(dims))])
    return factor_of


def normal_values(own_key, shape, spread, most, cuts=(), kind=jnp.bfloat16):
    result = jax.random.normal(own_key, shape, jnp.float32) * spread
    if len(cuts) > 0:
        result = shard_levels(own_key, shape, cuts, -0.22, 0.18) * result
    return jnp.clip(result, min=-most, max=most).astype(kind)


def setup_inputs(seed: int = 0) -> dict:
    streams_of = jax.random.split(jax.random.key(seed), 8)
    features = normal_values(streams_of[0], (NODES, FEAT), 1.0, 6.0, ((0, 256),))
    weight = normal_values(streams_of[1], (FEAT, HIDDEN_SIZE), FEAT ** -0.5, 0.5)
    grad_out = normal_values(streams_of[2], (NODES, HIDDEN_SIZE), 1.0, 6.0, ((0, 256),))
    tile_rows = set_ends(jax.random.randint(streams_of[3], (PROWS, PCOLS, NT), 0, ROW_BLOCKS), jax.random.fold_in(streams_of[3], 1), 0, ROW_BLOCKS - 1).astype(jnp.int32)
    tile_cols = set_ends(jax.random.randint(streams_of[4], (PROWS, PCOLS, NT), 0, COL_BLOCKS), jax.random.fold_in(streams_of[4], 1), 0, COL_BLOCKS - 1).astype(jnp.int32)
    tile_vals = draw_tile_vals(jax.random.fold_in(streams_of[7], 71), 0)
    tile_count = draw_tile_count(jax.random.fold_in(streams_of[7], 71), 0)
    return {"features": features, "weight": weight, "grad_out": grad_out, "tile_rows": tile_rows, "tile_cols": tile_cols, "tile_vals": tile_vals, "tile_count": tile_count}


def reference(features, weight, grad_out, tile_rows, tile_cols, tile_vals, tile_count):
    hidden_in = jnp.dot(features, weight, preferred_element_type=jnp.float32).astype(jnp.bfloat16)
    row_nodes = ROW_BLOCKS * BLOCK
    devs = PROWS * PCOLS
    flat_rows = tile_rows.reshape(devs, NT)
    flat_cols = tile_cols.reshape(devs, NT)
    flat_vals = tile_vals.reshape(devs, NT, BLOCK, BLOCK)
    flat_count = tile_count.reshape(devs)
    hidden4 = hidden_in.reshape(PROWS, PCOLS, NODE_DEV, HIDDEN_SIZE)
    slots = jnp.arange(NT, dtype=jnp.int32)

    def forward_step(carry, device):
        gi = (device // PCOLS).astype(jnp.int32)
        gj = (device % PCOLS).astype(jnp.int32)
        panel = lax.dynamic_slice(hidden4, (jnp.int32(0), gj, jnp.int32(0), jnp.int32(0)), (PROWS, 1, NODE_DEV, HIDDEN_SIZE))
        panel = panel.reshape(COL_BLOCKS, BLOCK, HIDDEN_SIZE)
        live = (slots < flat_count[device]).astype(jnp.float32)
        blocks = panel[flat_cols[device]].astype(jnp.float32)
        values = flat_vals[device].astype(jnp.float32)
        prod = jnp.einsum('tab,tbh->tah', values, blocks) * live[:, None, None]
        partial_value = jax.ops.segment_sum(prod, flat_rows[device], num_segments=ROW_BLOCKS).reshape(row_nodes, HIDDEN_SIZE)
        start = (gi * row_nodes).astype(jnp.int32)
        current = lax.dynamic_slice(carry, (start, jnp.int32(0)), (row_nodes, HIDDEN_SIZE))
        return lax.dynamic_update_slice(carry, current + partial_value, (start, jnp.int32(0))), None

    pre, _ = lax.scan(forward_step, jnp.zeros((NODES, HIDDEN_SIZE), jnp.float32), jnp.arange(devs, dtype=jnp.int32))
    sig = 1.0 / (1.0 + jnp.exp(-pre))
    activation = (pre * sig).astype(jnp.bfloat16)
    grad_pre = (grad_out.astype(jnp.float32) * sig * (1.0 + pre * (1.0 - sig))).astype(jnp.bfloat16)

    def backward_step(carry, device):
        gi = (device // PCOLS).astype(jnp.int32)
        gj = (device % PCOLS).astype(jnp.int32)
        rows_part = lax.dynamic_slice(grad_pre, ((gi * row_nodes).astype(jnp.int32), jnp.int32(0)), (row_nodes, HIDDEN_SIZE))
        rows_part = rows_part.reshape(ROW_BLOCKS, BLOCK, HIDDEN_SIZE)
        live = (slots < flat_count[device]).astype(jnp.float32)
        blocks = rows_part[flat_rows[device]].astype(jnp.float32)
        values = flat_vals[device].astype(jnp.float32)
        prod = jnp.einsum('tab,tah->tbh', values, blocks) * live[:, None, None]
        partial_value = jax.ops.segment_sum(prod, flat_cols[device], num_segments=COL_BLOCKS)
        partial_value = partial_value.reshape(PROWS, 1, NODE_DEV, HIDDEN_SIZE)
        anchor = (jnp.int32(0), gj, jnp.int32(0), jnp.int32(0))
        current = lax.dynamic_slice(carry, anchor, (PROWS, 1, NODE_DEV, HIDDEN_SIZE))
        return lax.dynamic_update_slice(carry, current + partial_value, anchor), None

    grad4, _ = lax.scan(backward_step, jnp.zeros((PROWS, PCOLS, NODE_DEV, HIDDEN_SIZE), jnp.float32), jnp.arange(devs, dtype=jnp.int32))
    grad_hidden = grad4.reshape(NODES, HIDDEN_SIZE).astype(jnp.bfloat16)
    grad_features = jnp.dot(grad_hidden, weight.T, preferred_element_type=jnp.float32).astype(jnp.bfloat16)
    grad_weight = jnp.dot(features.T, grad_hidden, preferred_element_type=jnp.float32)
    return activation, grad_features, grad_weight
```

```python
import functools

import jax
import jax.numpy as jnp
from jax import lax
from jax.experimental import pallas as pl
from jax.experimental.pallas import tpu as pltpu
from jax.sharding import PartitionSpec as P

BF16 = jnp.bfloat16
F32 = jnp.float32
NY, NXL, NC, NXH, NZ = 4, 2, 2, 2, 8
SHARD = 512
BLOCK = 128
VMEM_LIMIT = 40 * 1024 * 1024


def send_row(x, dy=0, dx=0, dc=0):
    perm = []
    for y in range(NY):
        for a in range(NXL):
            for c in range(NC):
                perm.append(((y * NXL + a) * NC + c, ((y + dy) % NY * NXL + (a ^ dx)) * NC + (c ^ dc)))
    return lax.ppermute(x, "row", perm)


def send_col(x, dh=0, dz=0):
    perm = []
    for h in range(NXH):
        for z in range(NZ):
            perm.append((h * NZ + z, (h ^ dh) * NZ + (z + dz) % NZ))
    return lax.ppermute(x, "col", perm)


def swap(x, axis, count, bit):
    return lax.ppermute(x, axis, [(i, i ^ bit) for i in range(count)])


def all_reduce(x):
    for bit in (1, 2, 4, 8):
        x = x + swap(x, "row", 16, bit)
    for bit in (8, 1, 2, 4):
        x = x + swap(x, "col", 16, bit)
    return x


def row_slots(blocks):
    me = lax.axis_index("col")
    owner = blocks // 4
    rel = ((owner // NZ) ^ (me // NZ)) * NZ + (owner % NZ - me % NZ) % NZ
    return rel * 4 + blocks % 4


def col_slots(blocks):
    me = lax.axis_index("row")
    owner = blocks // 4
    rel_c = (owner % 2) ^ (me % 2)
    rel_x = (owner // 2 % 2) ^ (me // 2 % 2)
    rel_y = (owner // 4 - me // 4) % NY
    return (rel_c * 8 + rel_x * 4 + rel_y) * 4 + blocks % 4


def tile_kernel(places, outs, left, *refs):
    n_in = len(places)
    src_ref, dst_ref, count_ref, vals_ref = refs[:4]
    panel_refs = refs[4:4 + n_in]
    out_refs = refs[4 + n_in:4 + n_in + len(outs)]
    panel, acc, sem = refs[4 + n_in + len(outs):]
    copies = []
    for ref, pieces in zip(panel_refs, places):
        start = 0
        for first, rows in pieces:
            copy = pltpu.make_async_copy(
                ref.at[pl.ds(start, rows)], panel.at[pl.ds(first, rows)], sem.at[len(copies)]
            )
            copy.start()
            copies.append(copy)
            start += rows
    acc[...] = jnp.zeros_like(acc)
    for copy in copies:
        copy.wait()
    count = count_ref[0]
    unroll = 4

    def step(i, carry):
        prods = []
        for u in range(unroll):
            t = i * unroll + u
            tile = vals_ref[t]
            block = panel[pl.ds(pl.multiple_of(src_ref[t] * BLOCK, BLOCK), BLOCK), :]
            a, b = (tile, block) if left else (block, tile)
            prod = jnp.dot(a, b, preferred_element_type=F32)
            prods.append(jnp.where(t < count, prod, 0.0))
        for u in range(unroll):
            at = pl.ds(pl.multiple_of(dst_ref[i * unroll + u] * BLOCK, BLOCK), BLOCK)
            acc[at, :] = acc[at, :] + prods[u]
        return carry

    lax.fori_loop(0, (count + unroll - 1) // unroll, step, 0)
    for ref, pieces in zip(out_refs, outs):
        start = 0
        for first, rows in pieces:
            ref[pl.ds(start, rows), :] = acc[pl.ds(first, rows), :].astype(ref.dtype)
            start += rows


def tile_sums(src, dst, count, vals, panels, places, outs, dtypes, left):
    sizes = [sum(rows for _, rows in pieces) for pieces in outs]
    vmem = pl.BlockSpec(memory_space=pltpu.VMEM)
    smem = pl.BlockSpec(memory_space=pltpu.SMEM)
    n_copies = sum(len(pieces) for pieces in places)
    return pl.pallas_call(
        functools.partial(tile_kernel, places, outs, left),
        out_shape=[jax.ShapeDtypeStruct((rows, BLOCK), dt) for rows, dt in zip(sizes, dtypes)],
        in_specs=[smem, smem, smem, vmem] + [pl.BlockSpec(memory_space=pl.ANY)] * len(panels),
        out_specs=[vmem] * len(outs),
        scratch_shapes=[
            pltpu.VMEM((16 * SHARD, BLOCK), BF16),
            pltpu.VMEM((16 * SHARD, BLOCK), F32),
            pltpu.SemaphoreType.DMA((n_copies,)),
        ],
        compiler_params=pltpu.CompilerParams(vmem_limit_bytes=VMEM_LIMIT),
    )(src, dst, count, vals, *panels)


def mid_kernel(own_ref, r1, r2, r3, r4, r5, weight_ref, gout_ref, act_ref, gt_ref, gw_ref):
    ax = own_ref[...]
    for r in (r1, r2, r3, r4, r5):
        ax = ax + r[...].astype(F32)
    high = ax.astype(BF16)
    low = (ax - high.astype(F32)).astype(BF16)
    weight = weight_ref[...]
    pre = jnp.dot(high, weight, preferred_element_type=F32) + jnp.dot(
        low, weight, preferred_element_type=F32
    )
    sig = 1.0 / (1.0 + jnp.exp(-pre))
    act_ref[...] = (pre * sig).astype(BF16)
    gp = (gout_ref[...].astype(F32) * sig * (1.0 + pre * (1.0 - sig))).astype(BF16)
    for q in range(SHARD // BLOCK):
        at = slice(q * BLOCK, (q + 1) * BLOCK)
        gt_ref[at, :] = lax.dot_general(
            weight, gp[at, :], (((1,), (1,)), ((), ())), preferred_element_type=F32
        ).astype(BF16)
    first = (((0,), (0,)), ((), ()))
    gw_ref[...] = lax.dot_general(high, gp, first, preferred_element_type=F32) + lax.dot_general(
        low, gp, first, preferred_element_type=F32
    )


def last_kernel(own_ref, w_ref, r1, r2, r3, out_ref):
    total = own_ref[...] + w_ref[:SHARD, :].astype(F32)
    for r in (r1, r2, r3):
        total = total + r[...].astype(F32)
    for q in range(SHARD // BLOCK):
        at = slice(q * BLOCK, (q + 1) * BLOCK)
        out_ref[at, :] = total[at, :].T.astype(BF16)


def add(*terms):
    return functools.reduce(lambda a, b: a + b, [t.astype(F32) for t in terms])


def body(features, weight, grad_out, tile_rows, tile_cols, tile_vals, tile_count):
    params = pltpu.CompilerParams(vmem_limit_bytes=VMEM_LIMIT)
    values = tile_vals[0, 0]
    count = tile_count[0]
    row_at = row_slots(tile_rows[0, 0])
    col_at = col_slots(tile_cols[0, 0])
    S = SHARD

    a = send_row(features, dx=1)
    u = send_row(features, dy=1)
    d = send_row(features, dy=-1)
    ud = jnp.concatenate([u, d])
    xa = jnp.concatenate([features, a])
    w = send_row(xa, dy=2)
    v = send_row(ud, dx=1)
    h1 = jnp.concatenate([xa, ud])
    h2 = jnp.concatenate([w, v])
    c1 = send_row(h1, dc=1)
    c2 = send_row(h2, dc=1)
    p1 = [(0, S), (4 * S, S), (3 * S, S), (1 * S, S)]
    p2 = [(2 * S, S), (6 * S, S), (7 * S, S), (5 * S, S)]
    other = lambda pieces: [(f + 8 * S, r) for f, r in pieces]
    places = [p1, p2, other(p1), other(p2)]

    O = lambda k: (k % 8 * S, S)
    X = lambda k: ((8 + k % 8) * S, S)
    outs = [[X(-3)], [X(3)], [X(4)], [O(1)], [O(-1)], [O(-3), X(-1)], [O(3), X(1)],
            [X(-2)], [X(2)], [O(4)], [X(0)], [O(2)], [O(-2)], [O(0)]]
    (x5, x3, x4, o1, o7, e, g, x6, x2, o4, x0, o2, o6, o0) = tile_sums(
        col_at, row_at, count, values, [h1, h2, c1, c2], places, outs,
        [BF16] * 7 + [F32] * 7, True,
    )
    r5 = send_col(x5, dz=-1)
    r3 = send_col(x3, dz=1)
    r4 = send_col(x4, dh=1)
    s1 = send_col(o1, dz=1)
    s7 = send_col(o7, dz=-1)
    re = send_col(e, dz=-1)
    rg = send_col(g, dz=1)
    q = jnp.concatenate([add(x2, r3).astype(BF16), add(x6, r5).astype(BF16)])
    rq = send_col(q, dh=1)
    o4 = add(o4, r4).astype(BF16)
    rh = send_col(o4[: S // 2], dz=2)
    ri = send_col(o4[S // 2:], dz=-2)
    x0 = add(x0, re[S:], rg[S:]).astype(BF16)
    rx = send_col(x0, dh=1)
    zero = jnp.zeros((S // 2, BLOCK), F32)
    o2 = add(o2, rg[:S], rq[:S], jnp.concatenate([rh.astype(F32), zero])).astype(BF16)
    o6 = add(o6, re[:S], rq[S:], jnp.concatenate([zero, ri.astype(F32)])).astype(BF16)
    s2 = send_col(o2, dz=2)
    s6 = send_col(o6, dz=-2)

    activation, gt, weight_part = pl.pallas_call(
        mid_kernel,
        out_shape=[
            jax.ShapeDtypeStruct((S, 256), BF16),
            jax.ShapeDtypeStruct((S, BLOCK), BF16),
            jax.ShapeDtypeStruct((BLOCK, 256), F32),
        ],
        compiler_params=params,
    )(o0, s1, s7, rx, s2, s6, weight, grad_out)
    grad_weight = all_reduce(weight_part)

    a = send_col(gt, dh=1)
    u = send_col(gt, dz=1)
    d = send_col(gt, dz=-1)
    u2 = send_col(gt, dz=2)
    d2 = send_col(gt, dz=-2)
    e = send_col(jnp.concatenate([u2, a]), dz=1)
    g = send_col(jnp.concatenate([d2, a]), dz=-1)
    f1 = send_col(u2[: S // 2], dz=2)
    f2 = send_col(d2[S // 2:], dz=-2)
    q = send_col(jnp.concatenate([u2, d2]), dh=1)
    f4 = jnp.concatenate([f1, f2])
    m = send_col(q[:S], dz=1)
    n = send_col(q[S:], dz=-1)
    l = send_col(f4, dh=1)
    panels = [gt, a, u, d, u2, d2, e, g, f4, q, m, n, l]
    places = [[O(0)], [X(0)], [O(-1)], [O(1)], [O(-2)], [O(2)], [O(-3), X(-1)], [O(3), X(1)],
              [O(4)], [X(-2), X(2)], [X(-3)], [X(3)], [X(4)]]

    k = lambda dy, dx: ((dx * 4 + dy % 4) * S, S)
    order = [k(0, 0), k(0, 1), k(1, 0), k(-1, 0), k(1, 1), k(-1, 1), k(2, 0), k(2, 1)]
    own, away = tile_sums(
        row_at, col_at, count, values, panels, places, [order, other(order)], [F32, BF16], False
    )
    own = own + send_row(away, dc=1).astype(F32)
    w = send_row(own[6 * S:].astype(BF16), dy=2)
    v = send_row(own[4 * S:6 * S].astype(BF16), dx=1)
    o = add(own[S:2 * S], w[S:]).astype(BF16)
    ud = add(own[2 * S:4 * S], v).astype(BF16)
    ro = send_row(o, dx=1)
    ru = send_row(ud[:S], dy=1)
    rd = send_row(ud[S:], dy=-1)
    grad_features = pl.pallas_call(
        last_kernel,
        out_shape=jax.ShapeDtypeStruct((S, BLOCK), BF16),
        compiler_params=params,
    )(own[:S], w, ro, ru, rd)
    return (activation, grad_features, grad_weight)


def solution(mesh):
    return jax.shard_map(
        body,
        mesh=mesh,
        in_specs=(
            P(("row", "col"), None),
            P(),
            P(("row", "col"), None),
            P("row", "col", None),
            P("row", "col", None),
            P("row", "col", None, None, None),
            P("row", "col"),
        ),
        out_specs=(P(("row", "col"), None), P(("row", "col"), None), P()),
        check_vma=False,
    )
```

```python
import functools

import jax
import jax.numpy as jnp
from jax import lax
from jax.experimental import pallas as pl
from jax.experimental.pallas import tpu as pltpu
from jax.sharding import PartitionSpec as P

BF16 = jnp.bfloat16
F32 = jnp.float32
NY, NXL, NC, NXH, NZ = 4, 2, 2, 2, 8
SHARD = 512
BLOCK = 128
ROWS = SHARD + BLOCK
VMEM_LIMIT = 40 * 1024 * 1024


def send_row(x, dy=0, dx=0, dc=0):
    perm = []
    for y in range(NY):
        for a in range(NXL):
            for c in range(NC):
                perm.append(((y * NXL + a) * NC + c, ((y + dy) % NY * NXL + (a ^ dx)) * NC + (c ^ dc)))
    return lax.ppermute(x, "row", perm)


def send_col(x, dh=0, dz=0):
    perm = []
    for h in range(NXH):
        for z in range(NZ):
            perm.append((h * NZ + z, (h ^ dh) * NZ + (z + dz) % NZ))
    return lax.ppermute(x, "col", perm)


def row_slots(blocks):
    me = lax.axis_index("col")
    owner = blocks // 4
    rel = ((owner // NZ) ^ (me // NZ)) * NZ + (owner % NZ - me % NZ) % NZ
    return rel * 4 + blocks % 4


def col_slots(blocks):
    me = lax.axis_index("row")
    owner = blocks // 4
    rel_c = (owner % 2) ^ (me % 2)
    rel_x = (owner // 2 % 2) ^ (me // 2 % 2)
    rel_y = (owner // 4 - me // 4) % NY
    return (rel_c * 8 + rel_x * 4 + rel_y) * 4 + blocks % 4


def tile_kernel(places, outs, left, *refs):
    n_in = len(places)
    src_ref, dst_ref, count_ref, scan_ref, vals_ref = refs[:5]
    panel_refs = refs[5:5 + n_in]
    *out_refs, panel, acc, sem = refs[5 + n_in:]
    copies = []
    for ref, pieces in zip(panel_refs, places):
        start = 0
        for first, rows in pieces:
            copy = pltpu.make_async_copy(
                ref.at[pl.ds(start, rows)], panel.at[pl.ds(first, rows)], sem.at[len(copies)]
            )
            copy.start()
            copies.append(copy)
            start += rows
    acc[...] = jnp.zeros_like(acc)
    for copy in copies:
        copy.wait()
    count = count_ref[0]
    unroll = 4

    def step(i, carry):
        prods = []
        for u in range(unroll):
            t = i * unroll + u
            tile = vals_ref[t]
            block = panel[pl.ds(pl.multiple_of(src_ref[t] * BLOCK, BLOCK), BLOCK), :]
            a, b = (tile, block) if left else (block, tile)
            prod = jnp.dot(a, b, preferred_element_type=F32)
            prods.append(jnp.where(t < count, prod, 0.0))
        for u in range(unroll):
            at = pl.ds(pl.multiple_of(dst_ref[i * unroll + u] * BLOCK, BLOCK), BLOCK)
            acc[at, :] = acc[at, :] + prods[u]
        return carry

    lax.fori_loop(0, (count + unroll - 1) // unroll, step, 0)
    for ref, pieces in zip(out_refs, outs):
        start = 0
        for first, rows in pieces:
            ref[pl.ds(start, rows), :] = acc[pl.ds(first, rows), :].astype(ref.dtype)
            start += rows
    if not left:
        share = jnp.zeros((BLOCK, BLOCK), F32)
        for i in range(16):
            at = pl.multiple_of(16 * SHARD + scan_ref[i] * BLOCK, BLOCK)
            share = share + panel[pl.ds(at, BLOCK), :].astype(F32)
        out_refs[-1][...] = share.astype(BF16)


def tile_sums(src, dst, count, scan, vals, panels, places, outs, dtypes, left):
    sizes = [sum(rows for _, rows in pieces) for pieces in outs]
    vmem = pl.BlockSpec(memory_space=pltpu.VMEM)
    smem = pl.BlockSpec(memory_space=pltpu.SMEM)
    n_copies = sum(len(pieces) for pieces in places)
    out_shape = [jax.ShapeDtypeStruct((rows, BLOCK), dt) for rows, dt in zip(sizes, dtypes)]
    if not left:
        out_shape.append(jax.ShapeDtypeStruct((BLOCK, BLOCK), BF16))
    return pl.pallas_call(
        functools.partial(tile_kernel, places, outs, left),
        out_shape=out_shape,
        in_specs=[smem] * 4 + [vmem] + [pl.BlockSpec(memory_space=pl.ANY)] * len(panels),
        out_specs=[vmem] * len(out_shape),
        scratch_shapes=[
            pltpu.VMEM((16 * (SHARD if left else ROWS), BLOCK), BF16),
            pltpu.VMEM((16 * SHARD, BLOCK), F32),
            pltpu.SemaphoreType.DMA((n_copies,)),
        ],
        compiler_params=pltpu.CompilerParams(vmem_limit_bytes=VMEM_LIMIT),
    )(src, dst, count, scan, vals, *panels)


def mid_kernel(core_ref, own_ref, r1, r2, r3, r4, r5, weight_ref, gout_ref, act_ref, gt_ref, keep_ref, give_ref, gw_ref):
    ax = own_ref[...]
    for r in (r1, r2, r3, r4, r5):
        ax = ax + r[...].astype(F32)
    high = ax.astype(BF16)
    low = (ax - high.astype(F32)).astype(BF16)
    weight = weight_ref[...]
    pre = jnp.dot(high, weight, preferred_element_type=F32) + jnp.dot(
        low, weight, preferred_element_type=F32
    )
    sig = 1.0 / (1.0 + jnp.exp(-pre))
    act_ref[...] = (pre * sig).astype(BF16)
    gp = (gout_ref[...].astype(F32) * sig * (1.0 + pre * (1.0 - sig))).astype(BF16)
    for q in range(SHARD // BLOCK):
        at = slice(q * BLOCK, (q + 1) * BLOCK)
        gt_ref[at, :] = lax.dot_general(
            weight, gp[at, :], (((1,), (1,)), ((), ())), preferred_element_type=F32
        ).astype(BF16)
    first = (((0,), (0,)), ((), ()))
    gw_ref[...] = lax.dot_general(high, gp, first, preferred_element_type=F32) + lax.dot_general(
        low, gp, first, preferred_element_type=F32
    )
    core = core_ref[0]
    half = BLOCK // 2
    for ref, which in ((keep_ref, core), (give_ref, 1 - core)):
        at = pl.ds(pl.multiple_of(which * half, half), half)
        ref[:half, :] = gw_ref[at, :BLOCK]
        ref[half:, :] = gw_ref[at, BLOCK:]


def last_kernel(own_ref, w_ref, r1, r2, r3, out_ref):
    total = own_ref[...] + w_ref[:SHARD, :].astype(F32)
    for r in (r1, r2, r3):
        total = total + r[:SHARD, :].astype(F32)
    for q in range(SHARD // BLOCK):
        at = slice(q * BLOCK, (q + 1) * BLOCK)
        out_ref[at, :] = total[at, :].T.astype(BF16)


def add(*terms):
    return functools.reduce(lambda a, b: a + b, [t.astype(F32) for t in terms])


def rounded(x):
    return lax.reduce_precision(x, 8, 7)


def body(features, weight, grad_out, tile_rows, tile_cols, tile_vals, tile_count):
    params = pltpu.CompilerParams(vmem_limit_bytes=VMEM_LIMIT)
    values = tile_vals[0, 0]
    count = tile_count[0]
    row_at = row_slots(tile_rows[0, 0])
    col_at = col_slots(tile_cols[0, 0])
    core = lax.axis_index("row") % NC
    scan = row_slots(jnp.arange(16, dtype=jnp.int32) * 4) // 4
    S = SHARD

    a = send_row(features, dx=1)
    u = send_row(features, dy=1)
    d = send_row(features, dy=-1)
    ud = jnp.concatenate([u, d])
    xa = jnp.concatenate([features, a])
    w = send_row(xa, dy=2)
    v = send_row(ud, dx=1)
    h1 = jnp.concatenate([xa, ud])
    h2 = jnp.concatenate([w, v])
    c1 = send_row(h1, dc=1)
    c2 = send_row(h2, dc=1)
    p1 = [(0, S), (4 * S, S), (3 * S, S), (1 * S, S)]
    p2 = [(2 * S, S), (6 * S, S), (7 * S, S), (5 * S, S)]
    other = lambda pieces: [(f + 8 * S, r) for f, r in pieces]
    places = [p1, p2, other(p1), other(p2)]

    O = lambda k: (k % 8 * S, S)
    X = lambda k: ((8 + k % 8) * S, S)
    outs = [[X(-3)], [X(3)], [X(4)], [O(1)], [O(-1)], [O(-3), X(-1)], [O(3), X(1)],
            [X(-2)], [X(2)], [O(4)], [X(0)], [O(2)], [O(-2)], [O(0)]]
    (x5, x3, x4, o1, o7, e, g, x6, x2, o4, x0, o2, o6, o0) = tile_sums(
        col_at, row_at, count, scan, values, [h1, h2, c1, c2], places, outs,
        [BF16] * 7 + [F32] * 7, True,
    )
    r5 = send_col(x5, dz=-1)
    r3 = send_col(x3, dz=1)
    r4 = send_col(x4, dh=1)
    s1 = send_col(o1, dz=1)
    s7 = send_col(o7, dz=-1)
    re = send_col(e, dz=-1)
    rg = send_col(g, dz=1)
    q = jnp.concatenate([add(x2, r3).astype(BF16), add(x6, r5).astype(BF16)])
    rq = send_col(q, dh=1)
    o4 = add(o4, r4).astype(BF16)
    rh = send_col(o4[: S // 2], dz=2)
    ri = send_col(o4[S // 2:], dz=-2)
    x0 = add(x0, re[S:], rg[S:]).astype(BF16)
    rx = send_col(x0, dh=1)
    zero = jnp.zeros((S // 2, BLOCK), F32)
    o2 = add(o2, rg[:S], rq[:S], jnp.concatenate([rh.astype(F32), zero])).astype(BF16)
    o6 = add(o6, re[:S], rq[S:], jnp.concatenate([zero, ri.astype(F32)])).astype(BF16)
    s2 = send_col(o2, dz=2)
    s6 = send_col(o6, dz=-2)

    half = jax.ShapeDtypeStruct((BLOCK, BLOCK), F32)
    activation, gt, keep, give = pl.pallas_call(
        mid_kernel,
        out_shape=[
            jax.ShapeDtypeStruct((S, 256), BF16),
            jax.ShapeDtypeStruct((S, BLOCK), BF16),
            half,
            half,
        ],
        in_specs=[pl.BlockSpec(memory_space=pltpu.SMEM)] + [pl.BlockSpec(memory_space=pltpu.VMEM)] * 8,
        scratch_shapes=[pltpu.VMEM((BLOCK, 256), F32)],
        compiler_params=params,
    )(core[None], o0, s1, s7, rx, s2, s6, weight, grad_out)
    share = keep + send_row(give, dc=1)
    gt = jnp.concatenate([gt, share.astype(BF16)])

    a = send_col(gt, dh=1)
    u = send_col(gt, dz=1)
    d = send_col(gt, dz=-1)
    u2 = send_col(gt, dz=2)
    d2 = send_col(gt, dz=-2)
    e = send_col(jnp.concatenate([u2, a]), dz=1)
    g = send_col(jnp.concatenate([d2, a]), dz=-1)
    f1 = send_col(u2[: ROWS // 2], dz=2)
    f2 = send_col(d2[ROWS // 2:], dz=-2)
    q = send_col(jnp.concatenate([u2, d2]), dh=1)
    f4 = jnp.concatenate([f1, f2])
    m = send_col(q[:ROWS], dz=1)
    n = send_col(q[ROWS:], dz=-1)
    l = send_col(f4, dh=1)
    panels = [gt, a, u, d, u2, d2, e, g, f4, q, m, n, l]
    both = lambda *slots: [p for f, r in slots for p in ((f, r), (16 * S + f // 4, BLOCK))]
    places = [both(O(0)), both(X(0)), both(O(-1)), both(O(1)), both(O(-2)), both(O(2)),
              both(O(-3), X(-1)), both(O(3), X(1)), both(O(4)), both(X(-2), X(2)),
              both(X(-3)), both(X(3)), both(X(4))]

    k = lambda dy, dx: ((dx * 4 + dy % 4) * S, S)
    order = [k(0, 0), k(0, 1), k(1, 0), k(-1, 0), k(1, 1), k(-1, 1), k(2, 0), k(2, 1)]
    own, away, share = tile_sums(
        row_at, col_at, count, scan, values, panels, places, [order, other(order)], [F32, BF16], False
    )
    own = own + send_row(away, dc=1).astype(F32)
    w = send_row(jnp.concatenate([own[6 * S:].astype(BF16), share]), dy=2)
    v = send_row(jnp.concatenate([own[4 * S:6 * S].astype(BF16), share]), dx=1)
    o = add(own[S:2 * S], w[S:2 * S]).astype(BF16)
    ud = add(own[2 * S:4 * S], v[:2 * S]).astype(BF16)
    here = rounded(add(share, w[2 * S:]))
    across = v[2 * S:]
    ro = send_row(jnp.concatenate([o, here.astype(BF16)]), dx=1)
    ru = send_row(jnp.concatenate([ud[:S], here.astype(BF16), across]), dy=1)
    rd = send_row(jnp.concatenate([ud[S:], across]), dy=-1)
    beside = rounded(add(ru[S + BLOCK:], rd[S:]))
    mine = add(here, ru[S:S + BLOCK]) + add(ro[S:], beside)
    theirs = send_row(mine, dc=1)
    grad_features = pl.pallas_call(
        last_kernel,
        out_shape=jax.ShapeDtypeStruct((S, BLOCK), BF16),
        compiler_params=params,
    )(own[:S], w, ro, ru, rd)
    wide = lambda x: jnp.concatenate([x[:BLOCK // 2], x[BLOCK // 2:]], axis=1)
    top, bottom = jnp.where(core == 0, mine, theirs), jnp.where(core == 0, theirs, mine)
    grad_weight = jnp.concatenate([wide(top), wide(bottom)])
    return (activation, grad_features, grad_weight)


def solution(mesh):
    return jax.shard_map(
        body,
        mesh=mesh,
        in_specs=(
            P(("row", "col"), None),
            P(),
            P(("row", "col"), None),
            P("row", "col", None),
            P("row", "col", None),
            P("row", "col", None, None, None),
            P("row", "col"),
        ),
        out_specs=(P(("row", "col"), None), P(("row", "col"), None), P()),
        check_vma=False,
    )
```

```python
import functools

import jax
import jax.numpy as jnp
from jax import lax
from jax.experimental import pallas as pl
from jax.experimental.pallas import tpu as pltpu
from jax.sharding import PartitionSpec as P

BF16 = jnp.bfloat16
F32 = jnp.float32
NY, NXL, NC, NXH, NZ = 4, 2, 2, 2, 8
SHARD = 512
BLOCK = 128
ROWS = SHARD + BLOCK
VMEM_LIMIT = 24 * 1024 * 1024


def send_row(x, dy=0, dx=0, dc=0):
    perm = []
    for y in range(NY):
        for a in range(NXL):
            for c in range(NC):
                perm.append(((y * NXL + a) * NC + c, ((y + dy) % NY * NXL + (a ^ dx)) * NC + (c ^ dc)))
    return lax.ppermute(x, "row", perm)


def send_col(x, dh=0, dz=0):
    perm = []
    for h in range(NXH):
        for z in range(NZ):
            perm.append((h * NZ + z, (h ^ dh) * NZ + (z + dz) % NZ))
    return lax.ppermute(x, "col", perm)


def row_slots(blocks):
    me = lax.axis_index("col")
    owner = blocks // 4
    rel = ((owner // NZ) ^ (me // NZ)) * NZ + (owner % NZ - me % NZ) % NZ
    return rel * 4 + blocks % 4


def col_slots(blocks):
    me = lax.axis_index("row")
    owner = blocks // 4
    rel_c = (owner % 2) ^ (me % 2)
    rel_x = (owner // 2 % 2) ^ (me // 2 % 2)
    rel_y = (owner // 4 - me // 4) % NY
    return (rel_c * 8 + rel_x * 4 + rel_y) * 4 + blocks % 4


def tile_kernel(places, outs, left, *refs):
    n_in = len(places)
    src_ref, dst_ref, count_ref, scan_ref, vals_ref = refs[:5]
    panel_refs = refs[5:5 + n_in]
    *out_refs, panel, acc = refs[5 + n_in:]
    for ref, pieces in zip(panel_refs, places):
        start = 0
        for first, rows in pieces:
            panel[pl.ds(first, rows), :] = ref[pl.ds(start, rows), :]
            start += rows
    acc[...] = jnp.zeros_like(acc)
    count = count_ref[0]
    unroll = 12

    def step(i, carry):
        prods = []
        for u in range(unroll):
            t = i * unroll + u
            tile = vals_ref[t]
            block = panel[pl.ds(pl.multiple_of(src_ref[t] * BLOCK, BLOCK), BLOCK), :]
            a, b = (tile, block) if left else (block, tile)
            prod = jnp.dot(a, b, preferred_element_type=F32)
            prods.append(jnp.where(t < count, prod, 0.0))
        for u in range(unroll):
            at = pl.ds(pl.multiple_of(dst_ref[i * unroll + u] * BLOCK, BLOCK), BLOCK)
            acc[at, :] = acc[at, :] + prods[u]
        return carry

    lax.fori_loop(0, (count + unroll - 1) // unroll, step, 0)
    for ref, pieces in zip(out_refs, outs):
        start = 0
        for first, rows in pieces:
            ref[pl.ds(start, rows), :] = acc[pl.ds(first, rows), :].astype(ref.dtype)
            start += rows
    if not left:
        share = jnp.zeros((BLOCK, BLOCK), F32)
        for i in range(16):
            at = pl.multiple_of(16 * SHARD + scan_ref[i] * BLOCK, BLOCK)
            share = share + panel[pl.ds(at, BLOCK), :].astype(F32)
        out_refs[-1][...] = share.astype(BF16)


def tile_sums(src, dst, count, scan, vals, panels, places, outs, dtypes, left):
    sizes = [sum(rows for _, rows in pieces) for pieces in outs]
    vmem = pl.BlockSpec(memory_space=pltpu.VMEM)
    smem = pl.BlockSpec(memory_space=pltpu.SMEM)
    out_shape = [jax.ShapeDtypeStruct((rows, BLOCK), dt) for rows, dt in zip(sizes, dtypes)]
    if not left:
        out_shape.append(jax.ShapeDtypeStruct((BLOCK, BLOCK), BF16))
    return pl.pallas_call(
        functools.partial(tile_kernel, places, outs, left),
        out_shape=out_shape,
        in_specs=[smem] * 4 + [vmem] * (1 + len(panels)),
        out_specs=[vmem] * len(out_shape),
        scratch_shapes=[
            pltpu.VMEM((16 * (SHARD if left else ROWS), BLOCK), BF16),
            pltpu.VMEM((16 * SHARD, BLOCK), F32),
        ],
        compiler_params=pltpu.CompilerParams(vmem_limit_bytes=VMEM_LIMIT),
    )(src, dst, count, scan, vals, *panels)


def mid_kernel(core_ref, own_ref, r1, r2, r3, r4, r5, weight_ref, gout_ref, act_ref, gt_ref, keep_ref, give_ref, gw_ref):
    ax = own_ref[...]
    for r in (r1, r2, r3, r4, r5):
        ax = ax + r[...].astype(F32)
    high = ax.astype(BF16)
    low = (ax - high.astype(F32)).astype(BF16)
    weight = weight_ref[...]
    pre = jnp.dot(high, weight, preferred_element_type=F32) + jnp.dot(
        low, weight, preferred_element_type=F32
    )
    sig = 1.0 / (1.0 + jnp.exp(-pre))
    act_ref[...] = (pre * sig).astype(BF16)
    gp = (gout_ref[...].astype(F32) * sig * (1.0 + pre * (1.0 - sig))).astype(BF16)
    for q in range(SHARD // BLOCK):
        at = slice(q * BLOCK, (q + 1) * BLOCK)
        gt_ref[at, :] = lax.dot_general(
            weight, gp[at, :], (((1,), (1,)), ((), ())), preferred_element_type=F32
        ).astype(BF16)
    first = (((0,), (0,)), ((), ()))
    gw_ref[...] = lax.dot_general(high, gp, first, preferred_element_type=F32) + lax.dot_general(
        low, gp, first, preferred_element_type=F32
    )
    core = core_ref[0]
    half = BLOCK // 2
    for ref, which in ((keep_ref, core), (give_ref, 1 - core)):
        at = pl.ds(pl.multiple_of(which * half, half), half)
        ref[:half, :] = gw_ref[at, :BLOCK]
        ref[half:, :] = gw_ref[at, BLOCK:]


def last_kernel(own_ref, w_ref, r1, r2, r3, out_ref):
    total = own_ref[...] + w_ref[:SHARD, :].astype(F32)
    for r in (r1, r2, r3):
        total = total + r[:SHARD, :].astype(F32)
    for q in range(SHARD // BLOCK):
        at = slice(q * BLOCK, (q + 1) * BLOCK)
        out_ref[at, :] = total[at, :].T.astype(BF16)


def add(*terms):
    return functools.reduce(lambda a, b: a + b, [t.astype(F32) for t in terms])


def rounded(x):
    return lax.reduce_precision(x, 8, 7)


def body(features, weight, grad_out, tile_rows, tile_cols, tile_vals, tile_count):
    params = pltpu.CompilerParams(vmem_limit_bytes=VMEM_LIMIT)
    values = tile_vals[0, 0]
    count = tile_count[0]
    row_at = row_slots(tile_rows[0, 0])
    col_at = col_slots(tile_cols[0, 0])
    core = lax.axis_index("row") % NC
    scan = row_slots(jnp.arange(16, dtype=jnp.int32) * 4) // 4
    S = SHARD

    a = send_row(features, dx=1)
    u = send_row(features, dy=1)
    d = send_row(features, dy=-1)
    ud = jnp.concatenate([u, d])
    xa = jnp.concatenate([features, a])
    w = send_row(xa, dy=2)
    v = send_row(ud, dx=1)
    h1 = jnp.concatenate([xa, ud])
    h2 = jnp.concatenate([w, v])
    c1 = send_row(h1, dc=1)
    c2 = send_row(h2, dc=1)
    p1 = [(0, S), (4 * S, S), (3 * S, S), (1 * S, S)]
    p2 = [(2 * S, S), (6 * S, S), (7 * S, S), (5 * S, S)]
    other = lambda pieces: [(f + 8 * S, r) for f, r in pieces]
    places = [p1, p2, other(p1), other(p2)]

    O = lambda k: (k % 8 * S, S)
    X = lambda k: ((8 + k % 8) * S, S)
    outs = [[X(-3)], [X(3)], [X(4)], [O(1)], [O(-1)], [O(-3), X(-1)], [O(3), X(1)],
            [X(-2)], [X(2)], [O(4)], [X(0)], [O(2)], [O(-2)], [O(0)]]
    (x5, x3, x4, o1, o7, e, g, x6, x2, o4, x0, o2, o6, o0) = tile_sums(
        col_at, row_at, count, scan, values, [h1, h2, c1, c2], places, outs,
        [BF16] * 7 + [F32] * 7, True,
    )
    r5 = send_col(x5, dz=-1)
    r3 = send_col(x3, dz=1)
    r4 = send_col(x4, dh=1)
    s1 = send_col(o1, dz=1)
    s7 = send_col(o7, dz=-1)
    re = send_col(e, dz=-1)
    rg = send_col(g, dz=1)
    q = jnp.concatenate([add(x2, r3).astype(BF16), add(x6, r5).astype(BF16)])
    rq = send_col(q, dh=1)
    o4 = add(o4, r4).astype(BF16)
    rh = send_col(o4[: S // 2], dz=2)
    ri = send_col(o4[S // 2:], dz=-2)
    x0 = add(x0, re[S:], rg[S:]).astype(BF16)
    rx = send_col(x0, dh=1)
    zero = jnp.zeros((S // 2, BLOCK), F32)
    o2 = add(o2, rg[:S], rq[:S], jnp.concatenate([rh.astype(F32), zero])).astype(BF16)
    o6 = add(o6, re[:S], rq[S:], jnp.concatenate([zero, ri.astype(F32)])).astype(BF16)
    s2 = send_col(o2, dz=2)
    s6 = send_col(o6, dz=-2)

    half = jax.ShapeDtypeStruct((BLOCK, BLOCK), F32)
    activation, gt, keep, give = pl.pallas_call(
        mid_kernel,
        out_shape=[
            jax.ShapeDtypeStruct((S, 256), BF16),
            jax.ShapeDtypeStruct((S, BLOCK), BF16),
            half,
            half,
        ],
        in_specs=[pl.BlockSpec(memory_space=pltpu.SMEM)] + [pl.BlockSpec(memory_space=pltpu.VMEM)] * 8,
        scratch_shapes=[pltpu.VMEM((BLOCK, 256), F32)],
        compiler_params=params,
    )(core[None], o0, s1, s7, rx, s2, s6, weight, grad_out)
    share = keep + send_row(give, dc=1)
    gt = jnp.concatenate([gt, share.astype(BF16)])

    a = send_col(gt, dh=1)
    u = send_col(gt, dz=1)
    d = send_col(gt, dz=-1)
    u2 = send_col(gt, dz=2)
    d2 = send_col(gt, dz=-2)
    e = send_col(jnp.concatenate([u2, a]), dz=1)
    g = send_col(jnp.concatenate([d2, a]), dz=-1)
    f1 = send_col(u2[: ROWS // 2], dz=2)
    f2 = send_col(d2[ROWS // 2:], dz=-2)
    q = send_col(jnp.concatenate([u2, d2]), dh=1)
    f4 = jnp.concatenate([f1, f2])
    m = send_col(q[:ROWS], dz=1)
    n = send_col(q[ROWS:], dz=-1)
    l = send_col(f4, dh=1)
    panels = [gt, a, u, d, u2, d2, e, g, f4, q, m, n, l]
    both = lambda *slots: [p for f, r in slots for p in ((f, r), (16 * S + f // 4, BLOCK))]
    places = [both(O(0)), both(X(0)), both(O(-1)), both(O(1)), both(O(-2)), both(O(2)),
              both(O(-3), X(-1)), both(O(3), X(1)), both(O(4)), both(X(-2), X(2)),
              both(X(-3)), both(X(3)), both(X(4))]

    k = lambda dy, dx: ((dx * 4 + dy % 4) * S, S)
    order = [k(0, 0), k(0, 1), k(1, 0), k(-1, 0), k(1, 1), k(-1, 1), k(2, 0), k(2, 1)]
    own, away, share = tile_sums(
        row_at, col_at, count, scan, values, panels, places, [order, other(order)], [F32, BF16], False
    )
    own = own + send_row(away, dc=1).astype(F32)
    w = send_row(jnp.concatenate([own[6 * S:].astype(BF16), share]), dy=2)
    v = send_row(jnp.concatenate([own[4 * S:6 * S].astype(BF16), share]), dx=1)
    o = add(own[S:2 * S], w[S:2 * S]).astype(BF16)
    ud = add(own[2 * S:4 * S], v[:2 * S]).astype(BF16)
    here = rounded(add(share, w[2 * S:]))
    across = v[2 * S:]
    ro = send_row(jnp.concatenate([o, here.astype(BF16)]), dx=1)
    ru = send_row(jnp.concatenate([ud[:S], here.astype(BF16), across]), dy=1)
    rd = send_row(jnp.concatenate([ud[S:], across]), dy=-1)
    beside = rounded(add(ru[S + BLOCK:], rd[S:]))
    mine = add(here, ru[S:S + BLOCK]) + add(ro[S:], beside)
    theirs = send_row(mine, dc=1)
    grad_features = pl.pallas_call(
        last_kernel,
        out_shape=jax.ShapeDtypeStruct((S, BLOCK), BF16),
        compiler_params=params,
    )(own[:S], w, ro, ru, rd)
    wide = lambda x: jnp.concatenate([x[:BLOCK // 2], x[BLOCK // 2:]], axis=1)
    top, bottom = jnp.where(core == 0, mine, theirs), jnp.where(core == 0, theirs, mine)
    grad_weight = jnp.concatenate([wide(top), wide(bottom)])
    return (activation, grad_features, grad_weight)


def solution(mesh):
    return jax.shard_map(
        body,
        mesh=mesh,
        in_specs=(
            P(("row", "col"), None),
            P(),
            P(("row", "col"), None),
            P("row", "col", None),
            P("row", "col", None),
            P("row", "col", None, None, None),
            P("row", "col"),
        ),
        out_specs=(P(("row", "col"), None), P(("row", "col"), None), P()),
        check_vma=False,
    )
```

```python
import functools

import jax
import jax.numpy as jnp
from jax import lax
from jax.experimental import pallas as pl
from jax.experimental.pallas import tpu as pltpu
from jax.sharding import PartitionSpec as P

BF16 = jnp.bfloat16
F32 = jnp.float32
NY, NXL, NC, NXH, NZ = 4, 2, 2, 2, 8
SHARD = 512
BLOCK = 128
ROWS = SHARD + BLOCK
VMEM_LIMIT = 24 * 1024 * 1024


def send_row(x, dy=0, dx=0, dc=0):
    perm = []
    for y in range(NY):
        for a in range(NXL):
            for c in range(NC):
                perm.append(((y * NXL + a) * NC + c, ((y + dy) % NY * NXL + (a ^ dx)) * NC + (c ^ dc)))
    return lax.ppermute(x, "row", perm)


def send_col(x, dh=0, dz=0):
    perm = []
    for h in range(NXH):
        for z in range(NZ):
            perm.append((h * NZ + z, (h ^ dh) * NZ + (z + dz) % NZ))
    return lax.ppermute(x, "col", perm)


def send_apart(x, dz):
    perm = []
    for r in range(NY * NXL * NC):
        for h in range(NXH):
            for z in range(NZ):
                to = h * NZ + (z + (dz if r % NC == 0 else -dz)) % NZ
                perm.append(((r * NXH + h) * NZ + z, r * NXH * NZ + to))
    return lax.ppermute(x, ("row", "col"), perm)


def copy_kernel(x_ref, out_ref):
    out_ref[...] = x_ref[...]


def row_slots(blocks):
    me = lax.axis_index("col")
    owner = blocks // 4
    rel = ((owner // NZ) ^ (me // NZ)) * NZ + (owner % NZ - me % NZ) % NZ
    return rel * 4 + blocks % 4


def col_slots(blocks):
    me = lax.axis_index("row")
    owner = blocks // 4
    rel_c = (owner % 2) ^ (me % 2)
    rel_x = (owner // 2 % 2) ^ (me // 2 % 2)
    rel_y = (owner // 4 - me // 4) % NY
    return (rel_c * 8 + rel_x * 4 + rel_y) * 4 + blocks % 4


def tile_kernel(places, outs, left, *refs):
    n_in = len(places)
    src_ref, dst_ref, count_ref, scan_ref, vals_ref = refs[:5]
    panel_refs = refs[5:5 + n_in]
    *out_refs, panel, acc = refs[5 + n_in:]
    for ref, pieces in zip(panel_refs, places):
        start = 0
        for first, rows in pieces:
            panel[pl.ds(first, rows), :] = ref[pl.ds(start, rows), :]
            start += rows
    acc[...] = jnp.zeros_like(acc)
    count = count_ref[0]
    unroll = 12

    def step(i, carry):
        prods = []
        for u in range(unroll):
            t = i * unroll + u
            tile = vals_ref[t]
            block = panel[pl.ds(pl.multiple_of(src_ref[t] * BLOCK, BLOCK), BLOCK), :]
            a, b = (tile, block) if left else (block, tile)
            prod = jnp.dot(a, b, preferred_element_type=F32)
            prods.append(jnp.where(t < count, prod, 0.0))
        for u in range(unroll):
            at = pl.ds(pl.multiple_of(dst_ref[i * unroll + u] * BLOCK, BLOCK), BLOCK)
            acc[at, :] = acc[at, :] + prods[u]
        return carry

    lax.fori_loop(0, (count + unroll - 1) // unroll, step, 0)
    for ref, pieces in zip(out_refs, outs):
        start = 0
        for first, rows in pieces:
            ref[pl.ds(start, rows), :] = acc[pl.ds(first, rows), :].astype(ref.dtype)
            start += rows
    if not left:
        share = jnp.zeros((BLOCK, BLOCK), F32)
        for i in range(16):
            at = pl.multiple_of(16 * SHARD + scan_ref[i] * BLOCK, BLOCK)
            share = share + panel[pl.ds(at, BLOCK), :].astype(F32)
        out_refs[-1][...] = share.astype(BF16)


def tile_sums(src, dst, count, scan, vals, panels, places, outs, dtypes, left):
    sizes = [sum(rows for _, rows in pieces) for pieces in outs]
    vmem = pl.BlockSpec(memory_space=pltpu.VMEM)
    smem = pl.BlockSpec(memory_space=pltpu.SMEM)
    out_shape = [jax.ShapeDtypeStruct((rows, BLOCK), dt) for rows, dt in zip(sizes, dtypes)]
    if not left:
        out_shape.append(jax.ShapeDtypeStruct((BLOCK, BLOCK), BF16))
    return pl.pallas_call(
        functools.partial(tile_kernel, places, outs, left),
        out_shape=out_shape,
        in_specs=[smem] * 4 + [vmem] * (1 + len(panels)),
        out_specs=[vmem] * len(out_shape),
        scratch_shapes=[
            pltpu.VMEM((16 * (SHARD if left else ROWS), BLOCK), BF16),
            pltpu.VMEM((16 * SHARD, BLOCK), F32),
        ],
        compiler_params=pltpu.CompilerParams(vmem_limit_bytes=VMEM_LIMIT),
    )(src, dst, count, scan, vals, *panels)


def mid_kernel(core_ref, own_ref, r1, r2, r3, r4, r5, weight_ref, gout_ref, act_ref, gt_ref, keep_ref, give_ref, gw_ref):
    ax = own_ref[...]
    for r in (r1, r2, r3, r4, r5):
        ax = ax + r[:SHARD, :].astype(F32)
    high = ax.astype(BF16)
    low = (ax - high.astype(F32)).astype(BF16)
    weight = weight_ref[...]
    pre = jnp.dot(high, weight, preferred_element_type=F32) + jnp.dot(
        low, weight, preferred_element_type=F32
    )
    sig = 1.0 / (1.0 + jnp.exp(-pre))
    act_ref[...] = (pre * sig).astype(BF16)
    gp = (gout_ref[...].astype(F32) * sig * (1.0 + pre * (1.0 - sig))).astype(BF16)
    for q in range(SHARD // BLOCK):
        at = slice(q * BLOCK, (q + 1) * BLOCK)
        gt_ref[at, :] = lax.dot_general(
            weight, gp[at, :], (((1,), (1,)), ((), ())), preferred_element_type=F32
        ).astype(BF16)
    first = (((0,), (0,)), ((), ()))
    gw_ref[...] = lax.dot_general(high, gp, first, preferred_element_type=F32) + lax.dot_general(
        low, gp, first, preferred_element_type=F32
    )
    core = core_ref[0]
    for ref, which in ((keep_ref, core), (give_ref, 1 - core)):
        ref[...] = gw_ref[:, pl.ds(pl.multiple_of(which * BLOCK, BLOCK), BLOCK)]


def last_kernel(own_ref, w_ref, r1, r2, r3, out_ref):
    total = own_ref[...] + w_ref[:SHARD, :].astype(F32)
    for r in (r1, r2, r3):
        total = total + r[:SHARD, :].astype(F32)
    for q in range(SHARD // BLOCK):
        at = slice(q * BLOCK, (q + 1) * BLOCK)
        out_ref[at, :] = total[at, :].T.astype(BF16)


def add(*terms):
    return functools.reduce(lambda a, b: a + b, [t.astype(F32) for t in terms])


def rounded(x):
    return lax.reduce_precision(x, 8, 7)


def body(features, weight, grad_out, tile_rows, tile_cols, tile_vals, tile_count):
    params = pltpu.CompilerParams(vmem_limit_bytes=VMEM_LIMIT)
    values = tile_vals[0, 0]
    count = tile_count[0]
    row_at = row_slots(tile_rows[0, 0])
    col_at = col_slots(tile_cols[0, 0])
    core = lax.axis_index("row") % NC
    scan = row_slots(jnp.arange(16, dtype=jnp.int32) * 4) // 4
    S = SHARD

    a = send_row(features, dx=1)
    u = send_row(features, dy=1)
    d = send_row(features, dy=-1)
    ud = jnp.concatenate([u, d])
    near = pl.pallas_call(
        copy_kernel, out_shape=jax.ShapeDtypeStruct((S, BLOCK), BF16), compiler_params=params
    )(features)
    xa = jnp.concatenate([near, a])
    w = send_row(xa, dy=2)
    v = send_row(ud, dx=1)
    h1 = jnp.concatenate([xa, ud])
    h2 = jnp.concatenate([w, v])
    c1 = send_row(h1, dc=1)
    c2 = send_row(h2, dc=1)
    p1 = [(0, S), (4 * S, S), (3 * S, S), (1 * S, S)]
    p2 = [(2 * S, S), (6 * S, S), (7 * S, S), (5 * S, S)]
    other = lambda pieces: [(f + 8 * S, r) for f, r in pieces]
    places = [p1, p2, other(p1), other(p2)]

    O = lambda k: (k % 8 * S, S)
    X = lambda k: ((8 + k % 8) * S, S)
    outs = [[X(-1), X(-3)], [X(1), X(3)], [X(4)], [O(-1), O(-3)], [O(1), O(3)],
            [X(-2)], [X(2)], [O(4)], [X(0)], [O(2)], [O(-2)], [O(0)]]
    m, n, l, e, g, x6, x2, o4, x0, o2, o6, o0 = tile_sums(
        col_at, row_at, count, scan, values, [h1, h2, c1, c2], places, outs,
        [BF16] * 5 + [F32] * 7, True,
    )
    m = send_col(m, dz=-1)
    n = send_col(n, dz=1)
    l = send_col(l, dh=1)
    e = send_col(e, dz=-1)
    g = send_col(g, dz=1)
    q = jnp.concatenate([add(x2, n[S:]).astype(BF16), add(x6, m[S:]).astype(BF16)])
    q = send_col(q, dh=1)
    h = send_apart(add(o4, l).astype(BF16), -2).astype(F32)
    rx = send_col(add(x0, m[:S], n[:S]).astype(BF16), dh=1)
    o2 = add(o2, g[S:], q[:S], jnp.where(core == 0, 0.0, h)).astype(BF16)
    o6 = add(o6, e[S:], q[S:], jnp.where(core == 0, h, 0.0)).astype(BF16)
    s2 = send_col(o2, dz=2)
    s6 = send_col(o6, dz=-2)

    half = jax.ShapeDtypeStruct((BLOCK, BLOCK), F32)
    activation, gt, keep, give = pl.pallas_call(
        mid_kernel,
        out_shape=[
            jax.ShapeDtypeStruct((S, 256), BF16),
            jax.ShapeDtypeStruct((S, BLOCK), BF16),
            half,
            half,
        ],
        in_specs=[pl.BlockSpec(memory_space=pltpu.SMEM)] + [pl.BlockSpec(memory_space=pltpu.VMEM)] * 8,
        scratch_shapes=[pltpu.VMEM((BLOCK, 256), F32)],
        compiler_params=params,
    )(core[None], o0, e, g, rx, s2, s6, weight, grad_out)
    share = keep + send_row(give, dc=1)
    gt = jnp.concatenate([gt, share.astype(BF16)])

    u2 = send_col(gt, dz=2)
    d2 = send_col(gt, dz=-2)
    a = send_col(gt, dh=1)
    q = send_col(jnp.concatenate([u2, d2]), dh=1)
    f4 = send_apart(jnp.where(core == 0, u2, d2), 2)
    e = send_col(jnp.concatenate([gt, u2]), dz=1)
    g = send_col(jnp.concatenate([gt, d2]), dz=-1)
    m = send_col(jnp.concatenate([a, q[:ROWS]]), dz=1)
    n = send_col(jnp.concatenate([a, q[ROWS:]]), dz=-1)
    l = send_col(f4, dh=1)
    panels = [gt, a, u2, d2, q, f4, e, g, m, n, l]
    both = lambda *slots: [p for f, r in slots for p in ((f, r), (16 * S + f // 4, BLOCK))]
    places = [both(O(0)), both(X(0)), both(O(-2)), both(O(2)), both(X(-2), X(2)), both(O(4)),
              both(O(-1), O(-3)), both(O(1), O(3)), both(X(-1), X(-3)), both(X(1), X(3)), both(X(4))]

    k = lambda dy, dx: ((dx * 4 + dy % 4) * S, S)
    last = [k(0, 0), k(0, 1), k(1, 0), k(-1, 0)]
    early = [k(1, 1), k(-1, 1), k(2, 0), k(2, 1)]
    own, away, own1, away1, share = tile_sums(
        row_at, col_at, count, scan, values, panels, places,
        [last, other(last), early, other(early)], [F32, BF16] * 2, False,
    )
    own1 = add(own1, send_row(away1, dc=1)).astype(BF16)
    own = add(own, send_row(away, dc=1))
    w = send_row(jnp.concatenate([own1[2 * S:], share]), dy=2)
    v = send_row(jnp.concatenate([own1[:2 * S], share]), dx=1)
    o = add(own[S:2 * S], w[S:2 * S]).astype(BF16)
    ud = add(own[2 * S:4 * S], v[:2 * S]).astype(BF16)
    here = rounded(add(share, w[2 * S:]))
    across = v[2 * S:]
    ro = send_row(jnp.concatenate([o, here.astype(BF16)]), dx=1)
    ru = send_row(jnp.concatenate([ud[:S], here.astype(BF16), across]), dy=1)
    rd = send_row(jnp.concatenate([ud[S:], across]), dy=-1)
    beside = rounded(add(ru[S + BLOCK:], rd[S:]))
    mine = add(here, ru[S:S + BLOCK]) + add(ro[S:], beside)
    theirs = send_row(mine, dc=1)
    grad_features = pl.pallas_call(
        last_kernel,
        out_shape=jax.ShapeDtypeStruct((S, BLOCK), BF16),
        compiler_params=params,
    )(own[:S], w, ro, ru, rd)
    first, second = jnp.where(core == 0, mine, theirs), jnp.where(core == 0, theirs, mine)
    grad_weight = jnp.concatenate([first, second], axis=1)
    return (activation, grad_features, grad_weight)


def solution(mesh):
    return jax.shard_map(
        body,
        mesh=mesh,
        in_specs=(
            P(("row", "col"), None),
            P(),
            P(("row", "col"), None),
            P("row", "col", None),
            P("row", "col", None),
            P("row", "col", None, None, None),
            P("row", "col"),
        ),
        out_specs=(P(("row", "col"), None), P(("row", "col"), None), P()),
        check_vma=False,
    )
```

```python
import functools

import jax
import jax.numpy as jnp
from jax import lax
from jax.experimental import pallas as pl
from jax.experimental.pallas import tpu as pltpu
from jax.sharding import PartitionSpec as P

BF16 = jnp.bfloat16
F32 = jnp.float32
NY, NXL, NC, NXH, NZ = 4, 2, 2, 2, 8
SHARD = 512
BLOCK = 128
VMEM_LIMIT = 16 * 1024 * 1024


def send_row(x, dy=0, dx=0, dc=0):
    perm = []
    for y in range(NY):
        for a in range(NXL):
            for c in range(NC):
                perm.append(((y * NXL + a) * NC + c, ((y + dy) % NY * NXL + (a ^ dx)) * NC + (c ^ dc)))
    return lax.ppermute(x, "row", perm)


def send_col(x, dh=0, dz=0):
    perm = []
    for h in range(NXH):
        for z in range(NZ):
            perm.append((h * NZ + z, (h ^ dh) * NZ + (z + dz) % NZ))
    return lax.ppermute(x, "col", perm)


def send_apart(x, dz):
    perm = []
    for r in range(NY * NXL * NC):
        for h in range(NXH):
            for z in range(NZ):
                to = h * NZ + (z + (dz if r % NC == 0 else -dz)) % NZ
                perm.append(((r * NXH + h) * NZ + z, r * NXH * NZ + to))
    return lax.ppermute(x, ("row", "col"), perm)


def copy_kernel(x_ref, out_ref):
    out_ref[...] = x_ref[...]


def row_slots(blocks):
    me = lax.axis_index("col")
    owner = blocks // 4
    rel = ((owner // NZ) ^ (me // NZ)) * NZ + (owner % NZ - me % NZ) % NZ
    return rel * 4 + blocks % 4


def col_slots(blocks):
    me = lax.axis_index("row")
    owner = blocks // 4
    rel_c = (owner % 2) ^ (me % 2)
    rel_x = (owner // 2 % 2) ^ (me // 2 % 2)
    rel_y = (owner // 4 - me // 4) % NY
    return (rel_c * 8 + rel_x * 4 + rel_y) * 4 + blocks % 4


def tile_kernel(places, outs, left, *refs):
    n_in = len(places)
    src_ref, dst_ref, count_ref, vals_ref = refs[:4]
    panel_refs = refs[4:4 + n_in]
    *out_refs, panel, acc = refs[4 + n_in:]
    for ref, pieces in zip(panel_refs, places):
        start = 0
        for first, rows in pieces:
            panel[pl.ds(first, rows), :] = ref[pl.ds(start, rows), :]
            start += rows
    acc[...] = jnp.zeros_like(acc)
    count = count_ref[0]
    unroll = 12

    def step(i, carry):
        prods = []
        for u in range(unroll):
            t = i * unroll + u
            tile = vals_ref[t]
            block = panel[pl.ds(pl.multiple_of(src_ref[t] * BLOCK, BLOCK), BLOCK), :]
            a, b = (tile, block) if left else (block, tile)
            prod = jnp.dot(a, b, preferred_element_type=F32)
            prods.append(jnp.where(t < count, prod, 0.0))
        for u in range(unroll):
            at = pl.ds(pl.multiple_of(dst_ref[i * unroll + u] * BLOCK, BLOCK), BLOCK)
            acc[at, :] = acc[at, :] + prods[u]
        return carry

    lax.fori_loop(0, (count + unroll - 1) // unroll, step, 0)
    for ref, pieces in zip(out_refs, outs):
        start = 0
        for first, rows in pieces:
            ref[pl.ds(start, rows), :] = acc[pl.ds(first, rows), :].astype(ref.dtype)
            start += rows


def tile_sums(src, dst, count, vals, panels, places, outs, dtypes, left):
    sizes = [sum(rows for _, rows in pieces) for pieces in outs]
    vmem = pl.BlockSpec(memory_space=pltpu.VMEM)
    smem = pl.BlockSpec(memory_space=pltpu.SMEM)
    out_shape = [jax.ShapeDtypeStruct((rows, BLOCK), dt) for rows, dt in zip(sizes, dtypes)]
    return pl.pallas_call(
        functools.partial(tile_kernel, places, outs, left),
        out_shape=out_shape,
        in_specs=[smem] * 3 + [vmem] * (1 + len(panels)),
        out_specs=[vmem] * len(out_shape),
        scratch_shapes=[
            pltpu.VMEM((16 * SHARD, BLOCK), BF16),
            pltpu.VMEM((16 * SHARD, BLOCK), F32),
        ],
        compiler_params=pltpu.CompilerParams(vmem_limit_bytes=VMEM_LIMIT),
    )(src, dst, count, vals, *panels)


def mid_kernel(core_ref, own_ref, r1, r2, r3, r4, r5, weight_ref, gout_ref, act_ref, gt_ref, keep_ref, give_ref, gw_ref):
    ax = own_ref[...]
    for r in (r1, r2, r3, r4, r5):
        ax = ax + r[:SHARD, :].astype(F32)
    high = ax.astype(BF16)
    low = (ax - high.astype(F32)).astype(BF16)
    weight = weight_ref[...]
    pre = jnp.dot(high, weight, preferred_element_type=F32) + jnp.dot(
        low, weight, preferred_element_type=F32
    )
    sig = 1.0 / (1.0 + jnp.exp(-pre))
    act_ref[...] = (pre * sig).astype(BF16)
    gp = (gout_ref[...].astype(F32) * sig * (1.0 + pre * (1.0 - sig))).astype(BF16)
    for q in range(SHARD // BLOCK):
        at = slice(q * BLOCK, (q + 1) * BLOCK)
        gt_ref[at, :] = lax.dot_general(
            weight, gp[at, :], (((1,), (1,)), ((), ())), preferred_element_type=F32
        ).astype(BF16)
    first = (((0,), (0,)), ((), ()))
    gw_ref[...] = lax.dot_general(high, gp, first, preferred_element_type=F32) + lax.dot_general(
        low, gp, first, preferred_element_type=F32
    )
    core = core_ref[0]
    for ref, which in ((keep_ref, core), (give_ref, 1 - core)):
        ref[...] = gw_ref[:, pl.ds(pl.multiple_of(which * BLOCK, BLOCK), BLOCK)]


def last_kernel(own_ref, w_ref, r1, r2, r3, out_ref):
    total = own_ref[...] + w_ref[:SHARD, :].astype(F32)
    for r in (r1, r2, r3):
        total = total + r[:SHARD, :].astype(F32)
    for q in range(SHARD // BLOCK):
        at = slice(q * BLOCK, (q + 1) * BLOCK)
        out_ref[at, :] = total[at, :].T.astype(BF16)


def add(*terms):
    return functools.reduce(lambda a, b: a + b, [t.astype(F32) for t in terms])


def swap(x, axis, bit):
    return lax.ppermute(x, axis, [(i, i ^ bit) for i in range(16)])


def tied(*arrays):
    return lax.optimization_barrier(arrays)


def body(features, weight, grad_out, tile_rows, tile_cols, tile_vals, tile_count):
    params = pltpu.CompilerParams(vmem_limit_bytes=VMEM_LIMIT)
    values = tile_vals[0, 0]
    count = tile_count[0]
    row_at = row_slots(tile_rows[0, 0])
    col_at = col_slots(tile_cols[0, 0])
    core = lax.axis_index("row") % NC
    S = SHARD

    a = send_row(features, dx=1)
    u = send_row(features, dy=1)
    d = send_row(features, dy=-1)
    ud = jnp.concatenate([u, d])
    near = pl.pallas_call(
        copy_kernel, out_shape=jax.ShapeDtypeStruct((S, BLOCK), BF16), compiler_params=params
    )(features)
    xa = jnp.concatenate([near, a])
    w = send_row(xa, dy=2)
    v = send_row(ud, dx=1)
    h1 = jnp.concatenate([xa, ud])
    h2 = jnp.concatenate([w, v])
    c1 = send_row(h1, dc=1)
    c2 = send_row(h2, dc=1)
    p1 = [(0, S), (4 * S, S), (3 * S, S), (1 * S, S)]
    p2 = [(2 * S, S), (6 * S, S), (7 * S, S), (5 * S, S)]
    other = lambda pieces: [(f + 8 * S, r) for f, r in pieces]
    places = [p1, p2, other(p1), other(p2)]

    O = lambda k: (k % 8 * S, S)
    X = lambda k: ((8 + k % 8) * S, S)
    outs = [[X(-3)], [X(3)], [X(4)], [O(-1), O(-3), X(-1)], [O(1), O(3), X(1)],
            [X(-2)], [X(2)], [O(4)], [X(0)], [O(2)], [O(-2)], [O(0)]]
    m, n, l, e, g, x6, x2, o4, x0, o2, o6, o0 = tile_sums(
        col_at, row_at, count, values, [h1, h2, c1, c2], places, outs,
        [BF16] * 5 + [F32] * 7, True,
    )
    m = send_col(m, dz=-1)
    n = send_col(n, dz=1)
    l = send_col(l, dh=1)
    e = send_col(e, dz=-1)
    g = send_col(g, dz=1)
    q = jnp.concatenate([add(x2, n).astype(BF16), add(x6, m).astype(BF16)])
    q = send_col(q, dh=1)
    h = send_apart(add(o4, l).astype(BF16), -2).astype(F32)
    rx = send_col(add(x0, e[2 * S:], g[2 * S:]).astype(BF16), dh=1)
    o2 = add(o2, g[S:2 * S], q[:S], jnp.where(core == 0, 0.0, h)).astype(BF16)
    o6 = add(o6, e[S:2 * S], q[S:], jnp.where(core == 0, h, 0.0)).astype(BF16)
    s2 = send_col(o2, dz=2)
    s6 = send_col(o6, dz=-2)

    half = jax.ShapeDtypeStruct((BLOCK, BLOCK), F32)
    activation, gt, keep, give = pl.pallas_call(
        mid_kernel,
        out_shape=[
            jax.ShapeDtypeStruct((S, 256), BF16),
            jax.ShapeDtypeStruct((S, BLOCK), BF16),
            half,
            half,
        ],
        in_specs=[pl.BlockSpec(memory_space=pltpu.SMEM)] + [pl.BlockSpec(memory_space=pltpu.VMEM)] * 8,
        scratch_shapes=[pltpu.VMEM((BLOCK, 256), F32)],
        compiler_params=params,
    )(core[None], o0, e, g, rx, s2, s6, weight, grad_out)
    share = keep + send_row(give, dc=1)

    u2 = send_col(gt, dz=2)
    d2 = send_col(gt, dz=-2)
    a = send_col(gt, dh=1)
    share = share + swap(share, "row", 2)
    share, u2, d2 = tied(share, u2, d2)
    share = share + swap(share, "row", 4)
    q = send_col(jnp.concatenate([u2, d2]), dh=1)
    f4 = send_apart(jnp.where(core == 0, u2, d2), 2)
    e = send_col(jnp.concatenate([gt, u2, a]), dz=1)
    g = send_col(jnp.concatenate([gt, d2, a]), dz=-1)
    share, f4 = tied(share, f4)
    share = share + swap(share, "row", 8)
    m = send_col(q[:S], dz=1)
    n = send_col(q[S:], dz=-1)
    l = send_col(f4, dh=1)
    share, e, g = tied(share, e, g)
    share = share + swap(share, "col", 8)
    panels = [gt, a, u2, d2, q, f4, e, g, m, n, l]
    places = [[O(0)], [X(0)], [O(-2)], [O(2)], [X(-2), X(2)], [O(4)],
              [O(-1), O(-3), X(-1)], [O(1), O(3), X(1)], [X(-3)], [X(3)], [X(4)]]

    k = lambda dy, dx: ((dx * 4 + dy % 4) * S, S)
    last = [k(0, 0), k(0, 1), k(1, 0), k(-1, 0)]
    early = [k(1, 1), k(-1, 1), k(2, 0), k(2, 1)]
    own, away, own1, away1 = tile_sums(
        row_at, col_at, count, values, panels, places,
        [last, other(last), early, other(early)], [F32, BF16] * 2, False,
    )
    own1 = add(own1, send_row(away1, dc=1)).astype(BF16)
    share, own1 = tied(share, own1)
    share = share + swap(share, "col", 4)
    own = add(own, send_row(away, dc=1))
    w = send_row(own1[2 * S:], dy=2)
    v = send_row(own1[:2 * S], dx=1)
    share, v = tied(share, v)
    for bit in (2, 1):
        share = share + swap(share, "col", bit)
    theirs = send_row(share, dc=1)
    o = add(own[S:2 * S], w[S:]).astype(BF16)
    ud = add(own[2 * S:], v).astype(BF16)
    ro = send_row(o, dx=1)
    ru = send_row(ud[:S], dy=1)
    rd = send_row(ud[S:], dy=-1)
    grad_features = pl.pallas_call(
        last_kernel,
        out_shape=jax.ShapeDtypeStruct((S, BLOCK), BF16),
        compiler_params=params,
    )(own[:S], w, ro, ru, rd)
    first, second = jnp.where(core == 0, share, theirs), jnp.where(core == 0, theirs, share)
    grad_weight = jnp.concatenate([first, second], axis=1)
    return (activation, grad_features, grad_weight)


def solution(mesh):
    return jax.shard_map(
        body,
        mesh=mesh,
        in_specs=(
            P(("row", "col"), None),
            P(),
            P(("row", "col"), None),
            P("row", "col", None),
            P("row", "col", None),
            P("row", "col", None, None, None),
            P("row", "col"),
        ),
        out_specs=(P(("row", "col"), None), P(("row", "col"), None), P()),
        check_vma=False,
    )
```

```python
import functools

import jax
import jax.numpy as jnp
from jax import lax
from jax.experimental import pallas as pl
from jax.experimental.pallas import tpu as pltpu
from jax.sharding import PartitionSpec as P

BF16 = jnp.bfloat16
F32 = jnp.float32
NY, NXL, NC, NXH, NZ = 4, 2, 2, 2, 8
SHARD = 512
BLOCK = 128
ROWS = SHARD + BLOCK
VMEM_LIMIT = 24 * 1024 * 1024


def tied(*arrays):
    return lax.optimization_barrier(arrays)


def send_row(x, dy=0, dx=0, dc=0):
    perm = []
    for y in range(NY):
        for a in range(NXL):
            for c in range(NC):
                perm.append(((y * NXL + a) * NC + c, ((y + dy) % NY * NXL + (a ^ dx)) * NC + (c ^ dc)))
    return lax.ppermute(x, "row", perm)


def send_col(x, dh=0, dz=0):
    perm = []
    for h in range(NXH):
        for z in range(NZ):
            perm.append((h * NZ + z, (h ^ dh) * NZ + (z + dz) % NZ))
    return lax.ppermute(x, "col", perm)


def send_apart(x, dz):
    perm = []
    for r in range(NY * NXL * NC):
        for h in range(NXH):
            for z in range(NZ):
                to = h * NZ + (z + (dz if r % NC == 0 else -dz)) % NZ
                perm.append(((r * NXH + h) * NZ + z, r * NXH * NZ + to))
    return lax.ppermute(x, ("row", "col"), perm)


def copy_kernel(x_ref, out_ref):
    out_ref[...] = x_ref[...]


def row_slots(blocks):
    me = lax.axis_index("col")
    owner = blocks // 4
    rel = ((owner // NZ) ^ (me // NZ)) * NZ + (owner % NZ - me % NZ) % NZ
    return rel * 4 + blocks % 4


def col_slots(blocks):
    me = lax.axis_index("row")
    owner = blocks // 4
    rel_c = (owner % 2) ^ (me % 2)
    rel_x = (owner // 2 % 2) ^ (me // 2 % 2)
    rel_y = (owner // 4 - me // 4) % NY
    return (rel_c * 8 + rel_x * 4 + rel_y) * 4 + blocks % 4


def tile_kernel(places, outs, left, *refs):
    n_in = len(places)
    src_ref, dst_ref, count_ref, scan_ref, vals_ref = refs[:5]
    panel_refs = refs[5:5 + n_in]
    *out_refs, panel, acc = refs[5 + n_in:]
    for ref, pieces in zip(panel_refs, places):
        start = 0
        for first, rows in pieces:
            panel[pl.ds(first, rows), :] = ref[pl.ds(start, rows), :]
            start += rows
    acc[...] = jnp.zeros_like(acc)
    count = count_ref[0]
    unroll = 12

    def step(i, carry):
        prods = []
        for u in range(unroll):
            t = i * unroll + u
            tile = vals_ref[t]
            block = panel[pl.ds(pl.multiple_of(src_ref[t] * BLOCK, BLOCK), BLOCK), :]
            a, b = (tile, block) if left else (block, tile)
            prod = jnp.dot(a, b, preferred_element_type=F32)
            prods.append(jnp.where(t < count, prod, 0.0))
        for u in range(unroll):
            at = pl.ds(pl.multiple_of(dst_ref[i * unroll + u] * BLOCK, BLOCK), BLOCK)
            acc[at, :] = acc[at, :] + prods[u]
        return carry

    lax.fori_loop(0, (count + unroll - 1) // unroll, step, 0)
    for ref, pieces in zip(out_refs, outs):
        start = 0
        for first, rows in pieces:
            ref[pl.ds(start, rows), :] = acc[pl.ds(first, rows), :].astype(ref.dtype)
            start += rows
    if not left:
        share = jnp.zeros((BLOCK, BLOCK), F32)
        for i in range(16):
            at = pl.multiple_of(16 * SHARD + scan_ref[i] * BLOCK, BLOCK)
            share = share + panel[pl.ds(at, BLOCK), :].astype(F32)
        out_refs[-1][...] = share.astype(BF16)


def tile_sums(src, dst, count, scan, vals, panels, places, outs, dtypes, left):
    sizes = [sum(rows for _, rows in pieces) for pieces in outs]
    vmem = pl.BlockSpec(memory_space=pltpu.VMEM)
    smem = pl.BlockSpec(memory_space=pltpu.SMEM)
    out_shape = [jax.ShapeDtypeStruct((rows, BLOCK), dt) for rows, dt in zip(sizes, dtypes)]
    if not left:
        out_shape.append(jax.ShapeDtypeStruct((BLOCK, BLOCK), BF16))
    return pl.pallas_call(
        functools.partial(tile_kernel, places, outs, left),
        out_shape=out_shape,
        in_specs=[smem] * 4 + [vmem] * (1 + len(panels)),
        out_specs=[vmem] * len(out_shape),
        scratch_shapes=[
            pltpu.VMEM((16 * (SHARD if left else ROWS), BLOCK), BF16),
            pltpu.VMEM((16 * SHARD, BLOCK), F32),
        ],
        compiler_params=pltpu.CompilerParams(vmem_limit_bytes=VMEM_LIMIT),
    )(src, dst, count, scan, vals, *panels)


def mid_kernel(core_ref, own_ref, r1, r2, r3, r4, r5, weight_ref, gout_ref, act_ref, gt_ref, keep_ref, give_ref, gw_ref):
    ax = own_ref[...]
    for r in (r1, r2, r3, r4, r5):
        ax = ax + r[:SHARD, :].astype(F32)
    high = ax.astype(BF16)
    low = (ax - high.astype(F32)).astype(BF16)
    weight = weight_ref[...]
    pre = jnp.dot(high, weight, preferred_element_type=F32) + jnp.dot(
        low, weight, preferred_element_type=F32
    )
    sig = 1.0 / (1.0 + jnp.exp(-pre))
    act_ref[...] = (pre * sig).astype(BF16)
    gp = (gout_ref[...].astype(F32) * sig * (1.0 + pre * (1.0 - sig))).astype(BF16)
    for q in range(SHARD // BLOCK):
        at = slice(q * BLOCK, (q + 1) * BLOCK)
        gt_ref[at, :] = lax.dot_general(
            weight, gp[at, :], (((1,), (1,)), ((), ())), preferred_element_type=F32
        ).astype(BF16)
    first = (((0,), (0,)), ((), ()))
    gw_ref[...] = lax.dot_general(high, gp, first, preferred_element_type=F32) + lax.dot_general(
        low, gp, first, preferred_element_type=F32
    )
    core = core_ref[0]
    for ref, which in ((keep_ref, core), (give_ref, 1 - core)):
        ref[...] = gw_ref[:, pl.ds(pl.multiple_of(which * BLOCK, BLOCK), BLOCK)]


def last_kernel(own_ref, w_ref, r1, r2, r3, out_ref):
    total = own_ref[...] + w_ref[:SHARD, :].astype(F32)
    for r in (r1, r2, r3):
        total = total + r[:SHARD, :].astype(F32)
    for q in range(SHARD // BLOCK):
        at = slice(q * BLOCK, (q + 1) * BLOCK)
        out_ref[at, :] = total[at, :].T.astype(BF16)


def add(*terms):
    return functools.reduce(lambda a, b: a + b, [t.astype(F32) for t in terms])


def rounded(x):
    return lax.reduce_precision(x, 8, 7)


def body(features, weight, grad_out, tile_rows, tile_cols, tile_vals, tile_count):
    params = pltpu.CompilerParams(vmem_limit_bytes=VMEM_LIMIT)
    values = tile_vals[0, 0]
    count = tile_count[0]
    row_at = row_slots(tile_rows[0, 0])
    col_at = col_slots(tile_cols[0, 0])
    core = lax.axis_index("row") % NC
    scan = row_slots(jnp.arange(16, dtype=jnp.int32) * 4) // 4
    S = SHARD

    a = send_row(features, dx=1)
    u = send_row(features, dy=1)
    d = send_row(features, dy=-1)
    near = pl.pallas_call(
        copy_kernel, out_shape=jax.ShapeDtypeStruct((S, BLOCK), BF16), compiler_params=params
    )(features)
    near, u, d = tied(near, u, d)
    ud = jnp.concatenate([u, d])
    xa = jnp.concatenate([near, a])
    w = send_row(xa, dy=2)
    v = send_row(ud, dx=1)
    h1 = jnp.concatenate([xa, ud])
    h2 = jnp.concatenate([w, v])
    c1 = send_row(h1, dc=1)
    c2 = send_row(h2, dc=1)
    p1 = [(0, S), (4 * S, S), (3 * S, S), (1 * S, S)]
    p2 = [(2 * S, S), (6 * S, S), (7 * S, S), (5 * S, S)]
    other = lambda pieces: [(f + 8 * S, r) for f, r in pieces]
    places = [p1, p2, other(p1), other(p2)]

    O = lambda k: (k % 8 * S, S)
    X = lambda k: ((8 + k % 8) * S, S)
    outs = [[X(-3)], [X(3)], [X(4)], [O(1)], [O(-1)], [O(-3), X(-1)], [O(3), X(1)],
            [X(-2)], [X(2)], [O(4)], [X(0)], [O(2)], [O(-2)], [O(0)]]
    (x5, x3, x4, o1, o7, e, g, x6, x2, o4, x0, o2, o6, o0) = tile_sums(
        col_at, row_at, count, scan, values, [h1, h2, c1, c2], places, outs,
        [BF16] * 7 + [F32] * 7, True,
    )
    r5 = send_col(x5, dz=-1)
    r3 = send_col(x3, dz=1)
    r4 = send_col(x4, dh=1)
    s1 = send_col(o1, dz=1)
    s7 = send_col(o7, dz=-1)
    re = send_col(e, dz=-1)
    rg = send_col(g, dz=1)
    q = jnp.concatenate([add(x2, r3).astype(BF16), add(x6, r5).astype(BF16)])
    rq = send_col(q, dh=1)
    o4 = add(o4, r4).astype(BF16)
    rh = send_col(o4[: S // 2], dz=2)
    ri = send_col(o4[S // 2:], dz=-2)
    x0 = add(x0, re[S:], rg[S:]).astype(BF16)
    rx = send_col(x0, dh=1)
    zero = jnp.zeros((S // 2, BLOCK), F32)
    o2 = add(o2, rg[:S], rq[:S], jnp.concatenate([rh.astype(F32), zero])).astype(BF16)
    o6 = add(o6, re[:S], rq[S:], jnp.concatenate([zero, ri.astype(F32)])).astype(BF16)
    s2 = send_col(o2, dz=2)
    s6 = send_col(o6, dz=-2)
    fin = (o0, s1, s7, rx, s2, s6)
    half = jax.ShapeDtypeStruct((BLOCK, BLOCK), F32)
    activation, gt, keep, give = pl.pallas_call(
        mid_kernel,
        out_shape=[
            jax.ShapeDtypeStruct((S, 256), BF16),
            jax.ShapeDtypeStruct((S, BLOCK), BF16),
            half,
            half,
        ],
        in_specs=[pl.BlockSpec(memory_space=pltpu.SMEM)] + [pl.BlockSpec(memory_space=pltpu.VMEM)] * 8,
        scratch_shapes=[pltpu.VMEM((BLOCK, 256), F32)],
        compiler_params=params,
    )(core[None], *fin, weight, grad_out)
    share = keep + send_row(give, dc=1)
    gt = jnp.concatenate([gt, share.astype(BF16)])

    u2 = send_col(gt, dz=2)
    d2 = send_col(gt, dz=-2)
    a = send_col(gt, dh=1)
    q = send_col(jnp.concatenate([u2, d2]), dh=1)
    f4 = send_apart(jnp.where(core == 0, u2, d2), 2)
    e = send_col(jnp.concatenate([gt, u2, a]), dz=1)
    g = send_col(jnp.concatenate([gt, d2, a]), dz=-1)
    m = send_col(q[:ROWS], dz=1)
    n = send_col(q[ROWS:], dz=-1)
    l = send_col(f4, dh=1)
    panels = [gt, a, u2, d2, q, f4, e, g, m, n, l]
    both = lambda *slots: [p for f, r in slots for p in ((f, r), (16 * S + f // 4, BLOCK))]
    places = [both(O(0)), both(X(0)), both(O(-2)), both(O(2)), both(X(-2), X(2)), both(O(4)),
              both(O(-1), O(-3), X(-1)), both(O(1), O(3), X(1)), both(X(-3)), both(X(3)), both(X(4))]

    k = lambda dy, dx: ((dx * 4 + dy % 4) * S, S)
    last = [k(0, 0), k(0, 1), k(1, 0), k(-1, 0)]
    early = [k(1, 1), k(-1, 1), k(2, 0), k(2, 1)]
    own, away, own1, away1, share = tile_sums(
        row_at, col_at, count, scan, values, panels, places,
        [last, other(last), early, other(early)], [F32, BF16] * 2, False,
    )
    own1 = add(own1, send_row(away1, dc=1)).astype(BF16)
    own = add(own, send_row(away, dc=1))
    w = send_row(jnp.concatenate([own1[2 * S:], share]), dy=2)
    v = send_row(jnp.concatenate([own1[:2 * S], share]), dx=1)

    o = add(own[S:2 * S], w[S:2 * S]).astype(BF16)
    ud = add(own[2 * S:4 * S], v[:2 * S]).astype(BF16)
    here = rounded(add(share, w[2 * S:]))
    across = v[2 * S:]
    ro = send_row(jnp.concatenate([o, here.astype(BF16)]), dx=1)
    ru = send_row(jnp.concatenate([ud[:S], here.astype(BF16), across]), dy=1)
    rd = send_row(jnp.concatenate([ud[S:], across]), dy=-1)
    beside = rounded(add(ru[S + BLOCK:], rd[S:]))
    mine = add(here, ru[S:S + BLOCK]) + add(ro[S:], beside)
    theirs = send_row(mine, dc=1)
    grad_features = pl.pallas_call(
        last_kernel,
        out_shape=jax.ShapeDtypeStruct((S, BLOCK), BF16),
        compiler_params=params,
    )(own[:S], w, ro, ru, rd)
    first, second = jnp.where(core == 0, mine, theirs), jnp.where(core == 0, theirs, mine)
    grad_weight = jnp.concatenate([first, second], axis=1)
    return (activation, grad_features, grad_weight)


def solution(mesh):
    return jax.shard_map(
        body,
        mesh=mesh,
        in_specs=(
            P(("row", "col"), None),
            P(),
            P(("row", "col"), None),
            P("row", "col", None),
            P("row", "col", None),
            P("row", "col", None, None, None),
            P("row", "col"),
        ),
        out_specs=(P(("row", "col"), None), P(("row", "col"), None), P()),
        check_vma=False,
    )
```

```python
import functools

import jax
import jax.numpy as jnp
from jax import lax
from jax.experimental import pallas as pl
from jax.experimental.pallas import tpu as pltpu
from jax.sharding import PartitionSpec as P

BF16 = jnp.bfloat16
F32 = jnp.float32
NY, NXL, NC, NXH, NZ = 4, 2, 2, 2, 8
SHARD = 512
BLOCK = 128
ROWS = SHARD + BLOCK
VMEM_LIMIT = 24 * 1024 * 1024


def tied(*arrays):
    return lax.optimization_barrier(arrays)


def send_row(x, dy=0, dx=0, dc=0):
    perm = []
    for y in range(NY):
        for a in range(NXL):
            for c in range(NC):
                perm.append(((y * NXL + a) * NC + c, ((y + dy) % NY * NXL + (a ^ dx)) * NC + (c ^ dc)))
    return lax.ppermute(x, "row", perm)


def send_col(x, dh=0, dz=0):
    perm = []
    for h in range(NXH):
        for z in range(NZ):
            perm.append((h * NZ + z, (h ^ dh) * NZ + (z + dz) % NZ))
    return lax.ppermute(x, "col", perm)


def send_apart(x, dz):
    perm = []
    for r in range(NY * NXL * NC):
        for h in range(NXH):
            for z in range(NZ):
                to = h * NZ + (z + (dz if r % NC == 0 else -dz)) % NZ
                perm.append(((r * NXH + h) * NZ + z, r * NXH * NZ + to))
    return lax.ppermute(x, ("row", "col"), perm)


def copy_kernel(x_ref, out_ref):
    out_ref[...] = x_ref[...]


def row_slots(blocks):
    me = lax.axis_index("col")
    owner = blocks // 4
    rel = ((owner // NZ) ^ (me // NZ)) * NZ + (owner % NZ - me % NZ) % NZ
    return rel * 4 + blocks % 4


def col_slots(blocks):
    me = lax.axis_index("row")
    owner = blocks // 4
    rel_c = (owner % 2) ^ (me % 2)
    rel_x = (owner // 2 % 2) ^ (me // 2 % 2)
    rel_y = (owner // 4 - me // 4) % NY
    return (rel_c * 8 + rel_x * 4 + rel_y) * 4 + blocks % 4


def tile_kernel(places, outs, left, *refs):
    n_in = len(places)
    src_ref, dst_ref, count_ref, scan_ref, vals_ref = refs[:5]
    panel_refs = refs[5:5 + n_in]
    *out_refs, panel, acc = refs[5 + n_in:]
    for ref, pieces in zip(panel_refs, places):
        start = 0
        for first, rows in pieces:
            panel[pl.ds(first, rows), :] = ref[pl.ds(start, rows), :]
            start += rows
    acc[...] = jnp.zeros_like(acc)
    count = count_ref[0]
    unroll = 12

    def step(i, carry):
        prods = []
        for u in range(unroll):
            t = i * unroll + u
            tile = vals_ref[t]
            block = panel[pl.ds(pl.multiple_of(src_ref[t] * BLOCK, BLOCK), BLOCK), :]
            a, b = (tile, block) if left else (block, tile)
            prod = jnp.dot(a, b, preferred_element_type=F32)
            prods.append(jnp.where(t < count, prod, 0.0))
        for u in range(unroll):
            at = pl.ds(pl.multiple_of(dst_ref[i * unroll + u] * BLOCK, BLOCK), BLOCK)
            acc[at, :] = acc[at, :] + prods[u]
        return carry

    lax.fori_loop(0, (count + unroll - 1) // unroll, step, 0)
    for ref, pieces in zip(out_refs, outs):
        start = 0
        for first, rows in pieces:
            ref[pl.ds(start, rows), :] = acc[pl.ds(first, rows), :].astype(ref.dtype)
            start += rows
    if not left:
        share = jnp.zeros((BLOCK, BLOCK), F32)
        for i in range(16):
            at = pl.multiple_of(16 * SHARD + scan_ref[i] * BLOCK, BLOCK)
            share = share + panel[pl.ds(at, BLOCK), :].astype(F32)
        out_refs[-1][...] = share.astype(BF16)


def tile_sums(src, dst, count, scan, vals, panels, places, outs, dtypes, left):
    sizes = [sum(rows for _, rows in pieces) for pieces in outs]
    vmem = pl.BlockSpec(memory_space=pltpu.VMEM)
    smem = pl.BlockSpec(memory_space=pltpu.SMEM)
    out_shape = [jax.ShapeDtypeStruct((rows, BLOCK), dt) for rows, dt in zip(sizes, dtypes)]
    if not left:
        out_shape.append(jax.ShapeDtypeStruct((BLOCK, BLOCK), BF16))
    return pl.pallas_call(
        functools.partial(tile_kernel, places, outs, left),
        out_shape=out_shape,
        in_specs=[smem] * 4 + [vmem] * (1 + len(panels)),
        out_specs=[vmem] * len(out_shape),
        scratch_shapes=[
            pltpu.VMEM((16 * (SHARD if left else ROWS), BLOCK), BF16),
            pltpu.VMEM((16 * SHARD, BLOCK), F32),
        ],
        compiler_params=pltpu.CompilerParams(vmem_limit_bytes=VMEM_LIMIT),
    )(src, dst, count, scan, vals, *panels)


def mid_kernel(core_ref, own_ref, r1, r2, r3, r4, r5, weight_ref, gout_ref, act_ref, gt_ref, keep_ref, give_ref, gw_ref):
    ax = own_ref[...]
    for r in (r1, r2, r3, r4, r5):
        ax = ax + r[:SHARD, :].astype(F32)
    high = ax.astype(BF16)
    low = (ax - high.astype(F32)).astype(BF16)
    weight = weight_ref[...]
    pre = jnp.dot(high, weight, preferred_element_type=F32) + jnp.dot(
        low, weight, preferred_element_type=F32
    )
    sig = 1.0 / (1.0 + jnp.exp(-pre))
    act_ref[...] = (pre * sig).astype(BF16)
    gp = (gout_ref[...].astype(F32) * sig * (1.0 + pre * (1.0 - sig))).astype(BF16)
    for q in range(SHARD // BLOCK):
        at = slice(q * BLOCK, (q + 1) * BLOCK)
        gt_ref[at, :] = lax.dot_general(
            weight, gp[at, :], (((1,), (1,)), ((), ())), preferred_element_type=F32
        ).astype(BF16)
    first = (((0,), (0,)), ((), ()))
    gw_ref[...] = lax.dot_general(high, gp, first, preferred_element_type=F32) + lax.dot_general(
        low, gp, first, preferred_element_type=F32
    )
    core = core_ref[0]
    for ref, which in ((keep_ref, core), (give_ref, 1 - core)):
        ref[...] = gw_ref[:, pl.ds(pl.multiple_of(which * BLOCK, BLOCK), BLOCK)]


def last_kernel(own_ref, w_ref, r1, r2, r3, out_ref):
    total = own_ref[...] + w_ref[:SHARD, :].astype(F32)
    for r in (r1, r2, r3):
        total = total + r[:SHARD, :].astype(F32)
    for q in range(SHARD // BLOCK):
        at = slice(q * BLOCK, (q + 1) * BLOCK)
        out_ref[at, :] = total[at, :].T.astype(BF16)


def join_kernel(a_ref, b_ref, c_ref, d_ref, out_ref):
    out_ref[:SHARD, :] = (a_ref[...] + b_ref[...].astype(F32)).astype(BF16)
    out_ref[SHARD:, :] = (c_ref[...] + d_ref[...].astype(F32)).astype(BF16)


def carry_kernel(core_ref, up_ref, down_ref, e_ref, g_ref, q_ref, h_ref, out_up, out_down):
    first = core_ref[0] == 0
    extra = h_ref[...].astype(F32)
    up = up_ref[...] + g_ref[SHARD:2 * SHARD, :].astype(F32) + q_ref[:SHARD, :].astype(F32)
    down = down_ref[...] + e_ref[SHARD:2 * SHARD, :].astype(F32) + q_ref[SHARD:, :].astype(F32)
    out_up[...] = (up + jnp.where(first, 0.0, extra)).astype(BF16)
    out_down[...] = (down + jnp.where(first, extra, 0.0)).astype(BF16)


def add(*terms):
    return functools.reduce(lambda a, b: a + b, [t.astype(F32) for t in terms])


def rounded(x):
    return lax.reduce_precision(x, 8, 7)


def body(features, weight, grad_out, tile_rows, tile_cols, tile_vals, tile_count):
    params = pltpu.CompilerParams(vmem_limit_bytes=VMEM_LIMIT)
    values = tile_vals[0, 0]
    count = tile_count[0]
    row_at = row_slots(tile_rows[0, 0])
    col_at = col_slots(tile_cols[0, 0])
    core = lax.axis_index("row") % NC
    scan = row_slots(jnp.arange(16, dtype=jnp.int32) * 4) // 4
    S = SHARD

    a = send_row(features, dx=1)
    u = send_row(features, dy=1)
    d = send_row(features, dy=-1)
    near = pl.pallas_call(
        copy_kernel, out_shape=jax.ShapeDtypeStruct((S, BLOCK), BF16), compiler_params=params
    )(features)
    near, u, d = tied(near, u, d)
    ud = jnp.concatenate([u, d])
    xa = jnp.concatenate([near, a])
    w = send_row(xa, dy=2)
    v = send_row(ud, dx=1)
    h1 = jnp.concatenate([xa, ud])
    h2 = jnp.concatenate([w, v])
    c1 = send_row(h1, dc=1)
    c2 = send_row(h2, dc=1)
    p1 = [(0, S), (4 * S, S), (3 * S, S), (1 * S, S)]
    p2 = [(2 * S, S), (6 * S, S), (7 * S, S), (5 * S, S)]
    other = lambda pieces: [(f + 8 * S, r) for f, r in pieces]
    places = [p1, p2, other(p1), other(p2)]

    O = lambda k: (k % 8 * S, S)
    X = lambda k: ((8 + k % 8) * S, S)
    outs = [[X(-3)], [X(3)], [X(4)], [O(-1), O(-3), X(-1)], [O(1), O(3), X(1)],
            [X(-2)], [X(2)], [O(4)], [X(0)], [O(2)], [O(-2)], [O(0)]]
    m, n, l, e, g, x6, x2, o4, x0, o2, o6, o0 = tile_sums(
        col_at, row_at, count, scan, values, [h1, h2, c1, c2], places, outs,
        [BF16] * 5 + [F32] * 7, True,
    )
    m = send_col(m, dz=-1)
    n = send_col(n, dz=1)
    l = send_col(l, dh=1)
    e = send_col(e, dz=-1)
    g = send_col(g, dz=1)
    q = pl.pallas_call(
        join_kernel, out_shape=jax.ShapeDtypeStruct((2 * S, BLOCK), BF16), compiler_params=params
    )(x2, n, x6, m)
    q = send_col(q, dh=1)
    h = send_apart(add(o4, l).astype(BF16), -2)
    rx = send_col(add(x0, e[2 * S:], g[2 * S:]).astype(BF16), dh=1)
    o2, o6 = pl.pallas_call(
        carry_kernel,
        out_shape=[jax.ShapeDtypeStruct((S, BLOCK), BF16)] * 2,
        in_specs=[pl.BlockSpec(memory_space=pltpu.SMEM)] + [pl.BlockSpec(memory_space=pltpu.VMEM)] * 6,
        compiler_params=params,
    )(core[None], o2, o6, e, g, q, h)
    s2 = send_col(o2, dz=2)
    s6 = send_col(o6, dz=-2)
    fin = (o0, e, g, rx, s2, s6)

    half = jax.ShapeDtypeStruct((BLOCK, BLOCK), F32)
    activation, gt, keep, give = pl.pallas_call(
        mid_kernel,
        out_shape=[
            jax.ShapeDtypeStruct((S, 256), BF16),
            jax.ShapeDtypeStruct((S, BLOCK), BF16),
            half,
            half,
        ],
        in_specs=[pl.BlockSpec(memory_space=pltpu.SMEM)] + [pl.BlockSpec(memory_space=pltpu.VMEM)] * 8,
        scratch_shapes=[pltpu.VMEM((BLOCK, 256), F32)],
        compiler_params=params,
    )(core[None], *fin, weight, grad_out)
    share = keep + send_row(give, dc=1)
    gt = jnp.concatenate([gt, share.astype(BF16)])

    u2 = send_col(gt, dz=2)
    d2 = send_col(gt, dz=-2)
    a = send_col(gt, dh=1)
    u = send_col(gt, dz=1)
    d = send_col(gt, dz=-1)
    q = send_col(jnp.concatenate([u2, d2]), dh=1)
    f4 = send_apart(jnp.where(core == 0, u2, d2), 2)
    e = send_col(jnp.concatenate([u2, a]), dz=1)
    g = send_col(jnp.concatenate([d2, a]), dz=-1)
    u, d, q = tied(u, d, q)
    m = send_col(q[:ROWS], dz=1)
    n = send_col(q[ROWS:], dz=-1)
    l = send_col(f4, dh=1)
    panels = [gt, a, u, d, u2, d2, q, f4, e, g, m, n, l]
    both = lambda *slots: [p for f, r in slots for p in ((f, r), (16 * S + f // 4, BLOCK))]
    places = [both(O(0)), both(X(0)), both(O(-1)), both(O(1)), both(O(-2)), both(O(2)), both(X(-2), X(2)),
              both(O(4)), both(O(-3), X(-1)), both(O(3), X(1)), both(X(-3)), both(X(3)), both(X(4))]

    k = lambda dy, dx: ((dx * 4 + dy % 4) * S, S)
    last = [k(0, 0), k(0, 1), k(1, 0), k(-1, 0)]
    early = [k(1, 1), k(-1, 1), k(2, 0), k(2, 1)]
    own, away, own1, away1, share = tile_sums(
        row_at, col_at, count, scan, values, panels, places,
        [last, other(last), early, other(early)], [F32, BF16] * 2, False,
    )
    own1 = add(own1, send_row(away1, dc=1)).astype(BF16)
    own = add(own, send_row(away, dc=1))
    w = send_row(jnp.concatenate([own1[2 * S:], share]), dy=2)
    v = send_row(jnp.concatenate([own1[:2 * S], share]), dx=1)

    o = add(own[S:2 * S], w[S:2 * S]).astype(BF16)
    ud = add(own[2 * S:4 * S], v[:2 * S]).astype(BF16)
    here = rounded(add(share, w[2 * S:]))
    across = v[2 * S:]
    ro = send_row(jnp.concatenate([o, here.astype(BF16)]), dx=1)
    ru = send_row(jnp.concatenate([ud[:S], here.astype(BF16), across]), dy=1)
    rd = send_row(jnp.concatenate([ud[S:], across]), dy=-1)
    beside = rounded(add(ru[S + BLOCK:], rd[S:]))
    mine = add(here, ru[S:S + BLOCK]) + add(ro[S:], beside)
    theirs = send_row(mine, dc=1)
    grad_features = pl.pallas_call(
        last_kernel,
        out_shape=jax.ShapeDtypeStruct((S, BLOCK), BF16),
        compiler_params=params,
    )(own[:S], w, ro, ru, rd)
    first, second = jnp.where(core == 0, mine, theirs), jnp.where(core == 0, theirs, mine)
    grad_weight = jnp.concatenate([first, second], axis=1)
    return (activation, grad_features, grad_weight)


def solution(mesh):
    return jax.shard_map(
        body,
        mesh=mesh,
        in_specs=(
            P(("row", "col"), None),
            P(),
            P(("row", "col"), None),
            P("row", "col", None),
            P("row", "col", None),
            P("row", "col", None, None, None),
            P("row", "col"),
        ),
        out_specs=(P(("row", "col"), None), P(("row", "col"), None), P()),
        check_vma=False,
    )
```

```python
import functools

import jax
import jax.numpy as jnp
from jax import lax
from jax.experimental import pallas as pl
from jax.experimental.pallas import tpu as pltpu
from jax.sharding import PartitionSpec as P

BF16 = jnp.bfloat16
F32 = jnp.float32
NY, NXL, NC, NXH, NZ = 4, 2, 2, 2, 8
SHARD = 512
BLOCK = 128
ROWS = SHARD + BLOCK
VMEM_LIMIT = 24 * 1024 * 1024


def tied(*arrays):
    return lax.optimization_barrier(arrays)


def send_row(x, dy=0, dx=0, dc=0):
    perm = []
    for y in range(NY):
        for a in range(NXL):
            for c in range(NC):
                perm.append(((y * NXL + a) * NC + c, ((y + dy) % NY * NXL + (a ^ dx)) * NC + (c ^ dc)))
    return lax.ppermute(x, "row", perm)


def send_col(x, dh=0, dz=0):
    perm = []
    for h in range(NXH):
        for z in range(NZ):
            perm.append((h * NZ + z, (h ^ dh) * NZ + (z + dz) % NZ))
    return lax.ppermute(x, "col", perm)


def send_apart(x, dz):
    perm = []
    for r in range(NY * NXL * NC):
        for h in range(NXH):
            for z in range(NZ):
                to = h * NZ + (z + (dz if r % NC == 0 else -dz)) % NZ
                perm.append(((r * NXH + h) * NZ + z, r * NXH * NZ + to))
    return lax.ppermute(x, ("row", "col"), perm)


def copy_kernel(x_ref, out_ref):
    out_ref[...] = x_ref[...]


def row_slots(blocks):
    me = lax.axis_index("col")
    owner = blocks // 4
    rel = ((owner // NZ) ^ (me // NZ)) * NZ + (owner % NZ - me % NZ) % NZ
    return rel * 4 + blocks % 4


def col_slots(blocks):
    me = lax.axis_index("row")
    owner = blocks // 4
    rel_c = (owner % 2) ^ (me % 2)
    rel_x = (owner // 2 % 2) ^ (me // 2 % 2)
    rel_y = (owner // 4 - me // 4) % NY
    return (rel_c * 8 + rel_x * 4 + rel_y) * 4 + blocks % 4


def tile_kernel(places, outs, left, *refs):
    n_in = len(places)
    src_ref, dst_ref, count_ref, scan_ref, vals_ref = refs[:5]
    panel_refs = refs[5:5 + n_in]
    *out_refs, panel, acc = refs[5 + n_in:]
    for ref, pieces in zip(panel_refs, places):
        start = 0
        for first, rows in pieces:
            panel[pl.ds(first, rows), :] = ref[pl.ds(start, rows), :]
            start += rows
    acc[...] = jnp.zeros_like(acc)
    count = count_ref[0]
    unroll = 16

    def step(i, carry):
        prods = []
        for u in range(unroll):
            t = i * unroll + u
            tile = vals_ref[t]
            block = panel[pl.ds(pl.multiple_of(src_ref[t] * BLOCK, BLOCK), BLOCK), :]
            a, b = (tile, block) if left else (block, tile)
            prod = jnp.dot(a, b, preferred_element_type=F32)
            prods.append(jnp.where(t < count, prod, 0.0))
        for u in range(unroll):
            at = pl.ds(pl.multiple_of(dst_ref[i * unroll + u] * BLOCK, BLOCK), BLOCK)
            acc[at, :] = acc[at, :] + prods[u]
        return carry

    lax.fori_loop(0, (count + unroll - 1) // unroll, step, 0)
    for ref, pieces in zip(out_refs, outs):
        start = 0
        for first, rows in pieces:
            ref[pl.ds(start, rows), :] = acc[pl.ds(first, rows), :].astype(ref.dtype)
            start += rows
    if not left:
        share = jnp.zeros((BLOCK, BLOCK), F32)
        for i in range(16):
            at = pl.multiple_of(16 * SHARD + scan_ref[i] * BLOCK, BLOCK)
            share = share + panel[pl.ds(at, BLOCK), :].astype(F32)
        out_refs[-1][...] = share.astype(BF16)


def tile_sums(src, dst, count, scan, vals, panels, places, outs, dtypes, left):
    sizes = [sum(rows for _, rows in pieces) for pieces in outs]
    vmem = pl.BlockSpec(memory_space=pltpu.VMEM)
    smem = pl.BlockSpec(memory_space=pltpu.SMEM)
    out_shape = [jax.ShapeDtypeStruct((rows, BLOCK), dt) for rows, dt in zip(sizes, dtypes)]
    if not left:
        out_shape.append(jax.ShapeDtypeStruct((BLOCK, BLOCK), BF16))
    return pl.pallas_call(
        functools.partial(tile_kernel, places, outs, left),
        out_shape=out_shape,
        in_specs=[smem] * 4 + [vmem] * (1 + len(panels)),
        out_specs=[vmem] * len(out_shape),
        scratch_shapes=[
            pltpu.VMEM((16 * (SHARD if left else ROWS), BLOCK), BF16),
            pltpu.VMEM((16 * SHARD, BLOCK), F32),
        ],
        compiler_params=pltpu.CompilerParams(vmem_limit_bytes=VMEM_LIMIT),
    )(src, dst, count, scan, vals, *panels)


def mid_kernel(core_ref, own_ref, r1, r2, r3, r4, r5, weight_ref, gout_ref, act_ref, gp_ref, keep_ref, give_ref, gw_ref):
    ax = own_ref[...]
    for r in (r1, r2, r3, r4, r5):
        ax = ax + r[:SHARD, :].astype(F32)
    high = ax.astype(BF16)
    low = (ax - high.astype(F32)).astype(BF16)
    weight = weight_ref[...]
    pre = jnp.dot(high, weight, preferred_element_type=F32) + jnp.dot(
        low, weight, preferred_element_type=F32
    )
    sig = 1.0 / (1.0 + jnp.exp(-pre))
    act_ref[...] = (pre * sig).astype(BF16)
    gp = (gout_ref[...].astype(F32) * sig * (1.0 + pre * (1.0 - sig))).astype(BF16)
    gp_ref[...] = gp
    first = (((0,), (0,)), ((), ()))
    gw_ref[...] = lax.dot_general(high, gp, first, preferred_element_type=F32) + lax.dot_general(
        low, gp, first, preferred_element_type=F32
    )
    core = core_ref[0]
    for ref, which in ((keep_ref, core), (give_ref, 1 - core)):
        ref[...] = gw_ref[:, pl.ds(pl.multiple_of(which * BLOCK, BLOCK), BLOCK)]


def back_kernel(gp_ref, weight_ref, gt_ref):
    gp, weight = gp_ref[...], weight_ref[...]
    for q in range(SHARD // BLOCK):
        at = slice(q * BLOCK, (q + 1) * BLOCK)
        gt_ref[at, :] = lax.dot_general(
            weight, gp[at, :], (((1,), (1,)), ((), ())), preferred_element_type=F32
        ).astype(BF16)


def last_kernel(own_ref, w_ref, r1, r2, r3, out_ref):
    total = own_ref[...] + w_ref[:SHARD, :].astype(F32)
    for r in (r1, r2, r3):
        total = total + r[:SHARD, :].astype(F32)
    for q in range(SHARD // BLOCK):
        at = slice(q * BLOCK, (q + 1) * BLOCK)
        out_ref[at, :] = total[at, :].T.astype(BF16)


def add(*terms):
    return functools.reduce(lambda a, b: a + b, [t.astype(F32) for t in terms])


def rounded(x):
    return lax.reduce_precision(x, 8, 7)


def body(features, weight, grad_out, tile_rows, tile_cols, tile_vals, tile_count):
    params = pltpu.CompilerParams(vmem_limit_bytes=VMEM_LIMIT)
    values = tile_vals[0, 0]
    count = tile_count[0]
    row_at = row_slots(tile_rows[0, 0])
    col_at = col_slots(tile_cols[0, 0])
    core = lax.axis_index("row") % NC
    scan = row_slots(jnp.arange(16, dtype=jnp.int32) * 4) // 4
    S = SHARD

    a = send_row(features, dx=1)
    u = send_row(features, dy=1)
    d = send_row(features, dy=-1)
    near = pl.pallas_call(
        copy_kernel, out_shape=jax.ShapeDtypeStruct((S, BLOCK), BF16), compiler_params=params
    )(features)
    near, u, d = tied(near, u, d)
    ud = jnp.concatenate([u, d])
    xa = jnp.concatenate([near, a])
    w = send_row(xa, dy=2)
    v = send_row(ud, dx=1)
    h1 = jnp.concatenate([xa, ud])
    h2 = jnp.concatenate([w, v])
    c1 = send_row(h1, dc=1)
    c2 = send_row(h2, dc=1)
    p1 = [(0, S), (4 * S, S), (3 * S, S), (1 * S, S)]
    p2 = [(2 * S, S), (6 * S, S), (7 * S, S), (5 * S, S)]
    other = lambda pieces: [(f + 8 * S, r) for f, r in pieces]
    places = [p1, p2, other(p1), other(p2)]

    O = lambda k: (k % 8 * S, S)
    X = lambda k: ((8 + k % 8) * S, S)
    outs = [[X(-3)], [X(3)], [X(4)], [O(1)], [O(-1)], [O(-3), X(-1)], [O(3), X(1)],
            [X(-2)], [X(2)], [O(4)], [X(0)], [O(2)], [O(-2)], [O(0)]]
    (x5, x3, x4, o1, o7, e, g, x6, x2, o4, x0, o2, o6, o0) = tile_sums(
        col_at, row_at, count, scan, values, [h1, h2, c1, c2], places, outs,
        [BF16] * 7 + [F32] * 7, True,
    )
    r5 = send_col(x5, dz=-1)
    r3 = send_col(x3, dz=1)
    r4 = send_col(x4, dh=1)
    s1 = send_col(o1, dz=1)
    s7 = send_col(o7, dz=-1)
    re = send_col(e, dz=-1)
    rg = send_col(g, dz=1)
    q = jnp.concatenate([add(x2, r3).astype(BF16), add(x6, r5).astype(BF16)])
    rq = send_col(q, dh=1)
    o4 = add(o4, r4).astype(BF16)
    rh = send_col(o4[: S // 2], dz=2)
    ri = send_col(o4[S // 2:], dz=-2)
    x0 = add(x0, re[S:], rg[S:]).astype(BF16)
    rx = send_col(x0, dh=1)
    zero = jnp.zeros((S // 2, BLOCK), F32)
    o2 = add(o2, rg[:S], rq[:S], jnp.concatenate([rh.astype(F32), zero])).astype(BF16)
    o6 = add(o6, re[:S], rq[S:], jnp.concatenate([zero, ri.astype(F32)])).astype(BF16)
    s2 = send_col(o2, dz=2)
    s6 = send_col(o6, dz=-2)
    fin = (o0, s1, s7, rx, s2, s6)
    half = jax.ShapeDtypeStruct((BLOCK, BLOCK), F32)
    activation, gp, keep, give = pl.pallas_call(
        mid_kernel,
        out_shape=[
            jax.ShapeDtypeStruct((S, 256), BF16),
            jax.ShapeDtypeStruct((S, 256), BF16),
            half,
            half,
        ],
        in_specs=[pl.BlockSpec(memory_space=pltpu.SMEM)] + [pl.BlockSpec(memory_space=pltpu.VMEM)] * 8,
        scratch_shapes=[pltpu.VMEM((BLOCK, 256), F32)],
        compiler_params=params,
    )(core[None], *fin, weight, grad_out)
    share = keep + send_row(give, dc=1)
    gt = pl.pallas_call(
        back_kernel, out_shape=jax.ShapeDtypeStruct((S, BLOCK), BF16), compiler_params=params
    )(gp, weight)
    gt = jnp.concatenate([gt, share.astype(BF16)])

    u2 = send_col(gt, dz=2)
    d2 = send_col(gt, dz=-2)
    a = send_col(gt, dh=1)
    q = send_col(jnp.concatenate([u2, d2]), dh=1)
    f4 = send_apart(jnp.where(core == 0, u2, d2), 2)
    e = send_col(jnp.concatenate([gt, u2, a]), dz=1)
    g = send_col(jnp.concatenate([gt, d2, a]), dz=-1)
    m = send_col(q[:ROWS], dz=1)
    n = send_col(q[ROWS:], dz=-1)
    l = send_col(f4, dh=1)
    panels = [gt, a, u2, d2, q, f4, e, g, m, n, l]
    both = lambda *slots: [p for f, r in slots for p in ((f, r), (16 * S + f // 4, BLOCK))]
    places = [both(O(0)), both(X(0)), both(O(-2)), both(O(2)), both(X(-2), X(2)), both(O(4)),
              both(O(-1), O(-3), X(-1)), both(O(1), O(3), X(1)), both(X(-3)), both(X(3)), both(X(4))]

    k = lambda dy, dx: ((dx * 4 + dy % 4) * S, S)
    last = [k(0, 0), k(0, 1), k(1, 0), k(-1, 0)]
    early = [k(1, 1), k(-1, 1), k(2, 0), k(2, 1)]
    own, away, own1, away1, share = tile_sums(
        row_at, col_at, count, scan, values, panels, places,
        [last, other(last), early, other(early)], [F32, BF16] * 2, False,
    )
    own1 = add(own1, send_row(away1, dc=1)).astype(BF16)
    own = add(own, send_row(away, dc=1))
    w = send_row(jnp.concatenate([own1[2 * S:], share]), dy=2)
    v = send_row(jnp.concatenate([own1[:2 * S], share]), dx=1)

    o = add(own[S:2 * S], w[S:2 * S]).astype(BF16)
    ud = add(own[2 * S:4 * S], v[:2 * S]).astype(BF16)
    here = rounded(add(share, w[2 * S:]))
    across = v[2 * S:]
    ro = send_row(jnp.concatenate([o, here.astype(BF16)]), dx=1)
    ru = send_row(jnp.concatenate([ud[:S], here.astype(BF16), across]), dy=1)
    rd = send_row(jnp.concatenate([ud[S:], across]), dy=-1)
    beside = rounded(add(ru[S + BLOCK:], rd[S:]))
    mine = add(here, ru[S:S + BLOCK]) + add(ro[S:], beside)
    theirs = send_row(mine, dc=1)
    grad_features = pl.pallas_call(
        last_kernel,
        out_shape=jax.ShapeDtypeStruct((S, BLOCK), BF16),
        compiler_params=params,
    )(own[:S], w, ro, ru, rd)
    first, second = jnp.where(core == 0, mine, theirs), jnp.where(core == 0, theirs, mine)
    grad_weight = jnp.concatenate([first, second], axis=1)
    return (activation, grad_features, grad_weight)


def solution(mesh):
    return jax.shard_map(
        body,
        mesh=mesh,
        in_specs=(
            P(("row", "col"), None),
            P(),
            P(("row", "col"), None),
            P("row", "col", None),
            P("row", "col", None),
            P("row", "col", None, None, None),
            P("row", "col"),
        ),
        out_specs=(P(("row", "col"), None), P(("row", "col"), None), P()),
        check_vma=False,
    )
```

```python
import functools

import jax
import jax.numpy as jnp
from jax import lax
from jax.experimental import pallas as pl
from jax.experimental.pallas import tpu as pltpu
from jax.sharding import PartitionSpec as P

BF16 = jnp.bfloat16
F32 = jnp.float32
NY, NXL, NC, NXH, NZ = 4, 2, 2, 2, 8
SHARD = 512
BLOCK = 128
ROWS = SHARD + BLOCK
VMEM_LIMIT = 24 * 1024 * 1024


def tied(*arrays):
    return lax.optimization_barrier(arrays)


def send_row(x, dy=0, dx=0, dc=0):
    perm = []
    for y in range(NY):
        for a in range(NXL):
            for c in range(NC):
                perm.append(((y * NXL + a) * NC + c, ((y + dy) % NY * NXL + (a ^ dx)) * NC + (c ^ dc)))
    return lax.ppermute(x, "row", perm)


def send_col(x, dh=0, dz=0):
    perm = []
    for h in range(NXH):
        for z in range(NZ):
            perm.append((h * NZ + z, (h ^ dh) * NZ + (z + dz) % NZ))
    return lax.ppermute(x, "col", perm)


def send_apart(x, dz):
    perm = []
    for r in range(NY * NXL * NC):
        for h in range(NXH):
            for z in range(NZ):
                to = h * NZ + (z + (dz if r % NC == 0 else -dz)) % NZ
                perm.append(((r * NXH + h) * NZ + z, r * NXH * NZ + to))
    return lax.ppermute(x, ("row", "col"), perm)


def copy_kernel(x_ref, out_ref):
    out_ref[...] = x_ref[...]


def row_slots(blocks):
    me = lax.axis_index("col")
    owner = blocks // 4
    rel = ((owner // NZ) ^ (me // NZ)) * NZ + (owner % NZ - me % NZ) % NZ
    return rel * 4 + blocks % 4


def col_slots(blocks):
    me = lax.axis_index("row")
    owner = blocks // 4
    rel_c = (owner % 2) ^ (me % 2)
    rel_x = (owner // 2 % 2) ^ (me // 2 % 2)
    rel_y = (owner // 4 - me // 4) % NY
    return (rel_c * 8 + rel_x * 4 + rel_y) * 4 + blocks % 4


def tile_kernel(places, outs, left, *refs):
    n_in = len(places)
    src_ref, dst_ref, count_ref, scan_ref, vals_ref = refs[:5]
    panel_refs = refs[5:5 + n_in]
    *out_refs, panel, acc = refs[5 + n_in:]
    for ref, pieces in zip(panel_refs, places):
        start = 0
        for first, rows in pieces:
            panel[pl.ds(first, rows), :] = ref[pl.ds(start, rows), :]
            start += rows
    acc[...] = jnp.zeros_like(acc)
    count = count_ref[0]
    unroll = 16

    def step(i, carry):
        prods = []
        for u in range(unroll):
            t = i * unroll + u
            tile = vals_ref[t]
            block = panel[pl.ds(pl.multiple_of(src_ref[t] * BLOCK, BLOCK), BLOCK), :]
            a, b = (tile, block) if left else (block, tile)
            prod = jnp.dot(a, b, preferred_element_type=F32)
            prods.append(jnp.where(t < count, prod, 0.0))
        for u in range(unroll):
            at = pl.ds(pl.multiple_of(dst_ref[i * unroll + u] * BLOCK, BLOCK), BLOCK)
            acc[at, :] = acc[at, :] + prods[u]
        return carry

    lax.fori_loop(0, (count + unroll - 1) // unroll, step, 0)
    for ref, pieces in zip(out_refs, outs):
        start = 0
        for first, rows in pieces:
            ref[pl.ds(start, rows), :] = acc[pl.ds(first, rows), :].astype(ref.dtype)
            start += rows
    if not left:
        share = jnp.zeros((BLOCK, BLOCK), F32)
        for i in range(16):
            at = pl.multiple_of(16 * SHARD + scan_ref[i] * BLOCK, BLOCK)
            share = share + panel[pl.ds(at, BLOCK), :].astype(F32)
        out_refs[-1][...] = share.astype(BF16)


def tile_sums(src, dst, count, scan, vals, panels, places, outs, dtypes, left):
    sizes = [sum(rows for _, rows in pieces) for pieces in outs]
    vmem = pl.BlockSpec(memory_space=pltpu.VMEM)
    smem = pl.BlockSpec(memory_space=pltpu.SMEM)
    out_shape = [jax.ShapeDtypeStruct((rows, BLOCK), dt) for rows, dt in zip(sizes, dtypes)]
    if not left:
        out_shape.append(jax.ShapeDtypeStruct((BLOCK, BLOCK), BF16))
    return pl.pallas_call(
        functools.partial(tile_kernel, places, outs, left),
        out_shape=out_shape,
        in_specs=[smem] * 4 + [vmem] * (1 + len(panels)),
        out_specs=[vmem] * len(out_shape),
        scratch_shapes=[
            pltpu.VMEM((16 * (SHARD if left else ROWS), BLOCK), BF16),
            pltpu.VMEM((16 * SHARD, BLOCK), F32),
        ],
        compiler_params=pltpu.CompilerParams(vmem_limit_bytes=VMEM_LIMIT),
    )(src, dst, count, scan, vals, *panels)


def mid_kernel(core_ref, own_ref, r1, r2, r3, r4, r5, weight_ref, gout_ref, act_ref, gp_ref, keep_ref, give_ref, gw_ref):
    ax = own_ref[...]
    for r in (r1, r2, r3, r4, r5):
        ax = ax + r[:SHARD, :].astype(F32)
    high = ax.astype(BF16)
    low = (ax - high.astype(F32)).astype(BF16)
    weight = weight_ref[...]
    pre = jnp.dot(high, weight, preferred_element_type=F32) + jnp.dot(
        low, weight, preferred_element_type=F32
    )
    sig = 1.0 / (1.0 + jnp.exp(-pre))
    act_ref[...] = (pre * sig).astype(BF16)
    gp = (gout_ref[...].astype(F32) * sig * (1.0 + pre * (1.0 - sig))).astype(BF16)
    gp_ref[...] = gp
    first = (((0,), (0,)), ((), ()))
    gw_ref[...] = lax.dot_general(high, gp, first, preferred_element_type=F32) + lax.dot_general(
        low, gp, first, preferred_element_type=F32
    )
    core = core_ref[0]
    for ref, which in ((keep_ref, core), (give_ref, 1 - core)):
        ref[...] = gw_ref[:, pl.ds(pl.multiple_of(which * BLOCK, BLOCK), BLOCK)]


def back_kernel(gp_ref, weight_ref, gt_ref):
    gp, weight = gp_ref[...], weight_ref[...]
    for q in range(SHARD // BLOCK):
        at = slice(q * BLOCK, (q + 1) * BLOCK)
        gt_ref[at, :] = lax.dot_general(
            weight, gp[at, :], (((1,), (1,)), ((), ())), preferred_element_type=F32
        ).astype(BF16)


def halves_kernel(core_ref, mine_ref, theirs_ref, out_ref):
    for ref, which in ((mine_ref, core_ref[0]), (theirs_ref, 1 - core_ref[0])):
        out_ref[:, pl.ds(pl.multiple_of(which * BLOCK, BLOCK), BLOCK)] = ref[...]


def last_kernel(own_ref, w_ref, r1, r2, r3, out_ref):
    total = own_ref[...] + w_ref[:SHARD, :].astype(F32)
    for r in (r1, r2, r3):
        total = total + r[:SHARD, :].astype(F32)
    for q in range(SHARD // BLOCK):
        at = slice(q * BLOCK, (q + 1) * BLOCK)
        out_ref[at, :] = total[at, :].T.astype(BF16)


def add(*terms):
    return functools.reduce(lambda a, b: a + b, [t.astype(F32) for t in terms])


def rounded(x):
    return lax.reduce_precision(x, 8, 7)


def body(features, weight, grad_out, tile_rows, tile_cols, tile_vals, tile_count):
    params = pltpu.CompilerParams(vmem_limit_bytes=VMEM_LIMIT)
    values = tile_vals[0, 0]
    count = tile_count[0]
    row_at = row_slots(tile_rows[0, 0])
    col_at = col_slots(tile_cols[0, 0])
    core = lax.axis_index("row") % NC
    scan = row_slots(jnp.arange(16, dtype=jnp.int32) * 4) // 4
    S = SHARD

    a = send_row(features, dx=1)
    u = send_row(features, dy=1)
    d = send_row(features, dy=-1)
    near = pl.pallas_call(
        copy_kernel, out_shape=jax.ShapeDtypeStruct((S, BLOCK), BF16), compiler_params=params
    )(features)
    near, u, d = tied(near, u, d)
    ud = jnp.concatenate([u, d])
    xa = jnp.concatenate([near, a])
    w = send_row(xa, dy=2)
    v = send_row(ud, dx=1)
    h1 = jnp.concatenate([xa, ud])
    h2 = jnp.concatenate([w, v])
    c1 = send_row(h1, dc=1)
    c2 = send_row(h2, dc=1)
    p1 = [(0, S), (4 * S, S), (3 * S, S), (1 * S, S)]
    p2 = [(2 * S, S), (6 * S, S), (7 * S, S), (5 * S, S)]
    other = lambda pieces: [(f + 8 * S, r) for f, r in pieces]
    places = [p1, p2, other(p1), other(p2)]

    O = lambda k: (k % 8 * S, S)
    X = lambda k: ((8 + k % 8) * S, S)
    outs = [[X(-3)], [X(3)], [X(4)], [O(1)], [O(-1)], [O(-3), X(-1)], [O(3), X(1)],
            [X(-2)], [X(2)], [O(4)], [X(0)], [O(2)], [O(-2)], [O(0)]]
    (x5, x3, x4, o1, o7, e, g, x6, x2, o4, x0, o2, o6, o0) = tile_sums(
        col_at, row_at, count, scan, values, [h1, h2, c1, c2], places, outs,
        [BF16] * 7 + [F32] * 7, True,
    )
    r5 = send_col(x5, dz=-1)
    r3 = send_col(x3, dz=1)
    r4 = send_col(x4, dh=1)
    s1 = send_col(o1, dz=1)
    s7 = send_col(o7, dz=-1)
    re = send_col(e, dz=-1)
    rg = send_col(g, dz=1)
    q = jnp.concatenate([add(x2, r3).astype(BF16), add(x6, r5).astype(BF16)])
    rq = send_col(q, dh=1)
    o4 = add(o4, r4).astype(BF16)
    rh = send_col(o4[: S // 2], dz=2)
    ri = send_col(o4[S // 2:], dz=-2)
    x0 = add(x0, re[S:], rg[S:]).astype(BF16)
    rx = send_col(x0, dh=1)
    zero = jnp.zeros((S // 2, BLOCK), F32)
    o2 = add(o2, rg[:S], rq[:S], jnp.concatenate([rh.astype(F32), zero])).astype(BF16)
    o6 = add(o6, re[:S], rq[S:], jnp.concatenate([zero, ri.astype(F32)])).astype(BF16)
    s2 = send_col(o2, dz=2)
    s6 = send_col(o6, dz=-2)
    fin = (o0, s1, s7, rx, s2, s6)
    half = jax.ShapeDtypeStruct((BLOCK, BLOCK), F32)
    activation, gp, keep, give = pl.pallas_call(
        mid_kernel,
        out_shape=[
            jax.ShapeDtypeStruct((S, 256), BF16),
            jax.ShapeDtypeStruct((S, 256), BF16),
            half,
            half,
        ],
        in_specs=[pl.BlockSpec(memory_space=pltpu.SMEM)] + [pl.BlockSpec(memory_space=pltpu.VMEM)] * 8,
        scratch_shapes=[pltpu.VMEM((BLOCK, 256), F32)],
        compiler_params=params,
    )(core[None], *fin, weight, grad_out)
    share = keep + send_row(give, dc=1)
    gt = pl.pallas_call(
        back_kernel, out_shape=jax.ShapeDtypeStruct((S, BLOCK), BF16), compiler_params=params
    )(gp, weight)
    gt = jnp.concatenate([gt, share.astype(BF16)])

    u2 = send_col(gt, dz=2)
    d2 = send_col(gt, dz=-2)
    a = send_col(gt, dh=1)
    q = send_col(jnp.concatenate([u2, d2]), dh=1)
    f4 = send_apart(jnp.where(core == 0, u2, d2), 2)
    e = send_col(jnp.concatenate([gt, u2, a]), dz=1)
    g = send_col(jnp.concatenate([gt, d2, a]), dz=-1)
    m = send_col(q[:ROWS], dz=1)
    n = send_col(q[ROWS:], dz=-1)
    l = send_col(f4, dh=1)
    panels = [gt, a, u2, d2, q, f4, e, g, m, n, l]
    both = lambda *slots: [p for f, r in slots for p in ((f, r), (16 * S + f // 4, BLOCK))]
    places = [both(O(0)), both(X(0)), both(O(-2)), both(O(2)), both(X(-2), X(2)), both(O(4)),
              both(O(-1), O(-3), X(-1)), both(O(1), O(3), X(1)), both(X(-3)), both(X(3)), both(X(4))]

    k = lambda dy, dx: ((dx * 4 + dy % 4) * S, S)
    last = [k(0, 0), k(0, 1), k(1, 0), k(-1, 0)]
    early = [k(1, 1), k(-1, 1), k(2, 0), k(2, 1)]
    own, away, own1, away1, share = tile_sums(
        row_at, col_at, count, scan, values, panels, places,
        [last, other(last), early, other(early)], [F32, BF16] * 2, False,
    )
    own1 = add(own1, send_row(away1, dc=1)).astype(BF16)
    own = add(own, send_row(away, dc=1))
    w = send_row(jnp.concatenate([own1[2 * S:], share]), dy=2)
    v = send_row(jnp.concatenate([own1[:2 * S], share]), dx=1)

    o = add(own[S:2 * S], w[S:2 * S]).astype(BF16)
    ud = add(own[2 * S:4 * S], v[:2 * S]).astype(BF16)
    here = rounded(add(share, w[2 * S:]))
    across = v[2 * S:]
    ro = send_row(jnp.concatenate([o, here.astype(BF16)]), dx=1)
    ru = send_row(jnp.concatenate([ud[:S], here.astype(BF16), across]), dy=1)
    rd = send_row(jnp.concatenate([ud[S:], across]), dy=-1)
    beside = rounded(add(ru[S + BLOCK:], rd[S:]))
    mine = add(here, ru[S:S + BLOCK]) + add(ro[S:], beside)
    theirs = send_row(mine, dc=1)
    grad_features = pl.pallas_call(
        last_kernel,
        out_shape=jax.ShapeDtypeStruct((S, BLOCK), BF16),
        compiler_params=params,
    )(own[:S], w, ro, ru, rd)
    grad_weight = pl.pallas_call(
        halves_kernel,
        out_shape=jax.ShapeDtypeStruct((BLOCK, 256), F32),
        in_specs=[pl.BlockSpec(memory_space=pltpu.SMEM)] + [pl.BlockSpec(memory_space=pltpu.VMEM)] * 2,
        compiler_params=params,
    )(core[None], mine, theirs)
    return (activation, grad_features, grad_weight)


def solution(mesh):
    return jax.shard_map(
        body,
        mesh=mesh,
        in_specs=(
            P(("row", "col"), None),
            P(),
            P(("row", "col"), None),
            P("row", "col", None),
            P("row", "col", None),
            P("row", "col", None, None, None),
            P("row", "col"),
        ),
        out_specs=(P(("row", "col"), None), P(("row", "col"), None), P()),
        check_vma=False,
    )
```
